256 devices in a mesh: dom: 32 (over x, y, core), head: 8 (over z).
Axes of the slice: x: 4, y: 4, z: 8, core: 2. Of those that a mesh axis runs over, the one named last changes fastest.
Arguments:
- feats: bfloat16 [32768, 256], P('dom'), may hold values from -15 to 15
- w_qkv: bfloat16 [3, 256, 256], P(None, None, 'head'), may hold values from -0.375 to 0.375
- w_out: bfloat16 [256, 256], P('head'), may hold values from -0.375 to 0.375
- virt_embed: bfloat16 [64, 256], replicated, may hold values from -6 to 6
- member: int32 [32768], P('dom'), may hold values from 0 to 63
- expander: int32 [32768, 2], P('dom'), may hold values from 0 to 32767, as said below
- local_mask: int32 [32768, 1024], P('dom'), may hold values from 0 to 1, as said below
- cotangent: bfloat16 [32768, 256], P('dom'), may hold values from -6 to 6
Outputs:
- mixed: bfloat16 [32768, 256], P('dom', 'head')
- grad_feats: bfloat16 [32768, 256], P('dom', 'head')
- grad_qkv: float32 [3, 256, 256], P(None, None, 'head')
- grad_out: float32 [256, 256], P('head')
- grad_virtual: float32 [64, 256], P(None, 'head')
The draws below stay inside these ranges and needn't reach their ends.
Inputs may be any that keep to these rules, and one draw needn't show every extreme that they name: Each column of expander is a permutation of the nodes; for the node at row r of its slab, expander[., e] lies in slab (r + e) mod 32. `local_mask`: every node's entry at its own column is 1.
All inputs are finite; a program needn't handle non-finite values.
Results may differ from the reference program's by a relative error of at most 0.009.
The reference program's roundings to bfloat16 on the way count: a program that leaves them out, or rounds other values in their place, can miss the bound.
Values may be sent and summed in bfloat16 or wider, within the bound.
No kernel may reach another device: no remote copies, remote signals or barrier semaphores. Data moves between devices by JAX's collectives and lax.ppermute only.
A program may use at most 64 MiB of HBM per device.

```python
import jax
import jax.numpy as jnp
from jax import lax

D = 256
H = 8
HD = 32
VIRT = 64
EXP = 2
TILE = 128
NDEV = 1024
SLABS = 32
NODES = 32768


def draw_feats(key, part):
    key = jax.random.fold_in(key, 11)
    base_key = jax.random.fold_in(key, 0)
    slab = (jnp.arange(NODES, dtype=jnp.int32) // NDEV).astype(jnp.float32)
    ramp = 1.0 + 2.0 * slab / max(SLABS - 1, 1)
    base = jnp.clip(jax.random.normal(base_key, (NODES, D), jnp.float32), -5.0, 5.0)
    return (base * ramp[:, None]).astype(jnp.bfloat16)


def draw_expander(key, part):
    key = jax.random.fold_in(key, 23)
    block = NDEV // SLABS
    subkeys = jax.random.split(key, EXP * SLABS)
    orders = jax.vmap(partial_permutation)(subkeys).reshape(EXP, SLABS, NDEV)
    rows = jnp.arange(NDEV, dtype=jnp.int32)
    sources = jnp.arange(SLABS, dtype=jnp.int32)
    columns = []
    for branch in range(EXP):
        target = (rows + branch) % SLABS
        slot = sources[:, None] * block + (rows // SLABS)[None, :]
        place = orders[branch][jnp.broadcast_to(target[None, :], (SLABS, NDEV)), slot]
        columns.append((target[None, :] * NDEV + place).reshape(NODES))
    return jnp.stack(columns, axis=1).astype(jnp.int32)


def partial_permutation(subkey):
    return jax.random.permutation(subkey, NDEV).astype(jnp.int32)


def draw_local_mask(key, part):
    key = jax.random.fold_in(key, 37)
    level_key, tile_key, entry_key = jax.random.split(key, 3)
    tiles = NDEV // TILE
    level = jnp.left_shift(jnp.int32(1), jax.random.randint(level_key, (SLABS, 1, 1), 0, 5))
    active = jax.random.randint(tile_key, (SLABS, tiles, tiles), 0, 16) < level
    active = active | jnp.eye(tiles, dtype=bool)[None]
    full_tiles = jnp.repeat(jnp.repeat(active, TILE, axis=1), TILE, axis=2)
    entries = jax.random.randint(entry_key, (SLABS, NDEV, NDEV), 0, 16) == 0
    chosen = entries & full_tiles | jnp.eye(NDEV, dtype=bool)[None]
    return chosen.astype(jnp.int32).reshape(NODES, NDEV)


def plant(values, key, least, largest):
    longest = values.shape.index(max(values.shape))
    spots = []
    for shift in (0, 1):
        where = [jax.random.randint(jax.random.fold_in(key, axis), (), 0, length) for axis, length in enumerate(values.shape)]
        where[longest] = (where[longest] + shift) % values.shape[longest]
        spots.append(tuple(where))
    return values.at[spots[0]].set(least).at[spots[1]].set(largest)


def block_levels(key, shape, shards, least, high):
    loudness = 1.0
    for axis_at, shards_of in shards:
        heights = jax.random.uniform(jax.random.fold_in(jax.random.fold_in(key, 6), axis_at), (shards_of,), jnp.float32, least / len(shards), high / len(shards))
        loudness = loudness * jnp.repeat(jnp.exp(heights), shape[axis_at] // shards_of).reshape((-1,) + (1,) * (len(shape) - 1 - axis_at))
    return loudness


def bell_draw(own_key, shape, scale, reach, cuts=(), kind=jnp.bfloat16):
    loudness = block_levels(own_key, shape, cuts, -0.22, 0.18) if cuts else 1.0
    array = jax.random.normal(own_key, shape, jnp.float32) * scale * loudness
    return jnp.minimum(jnp.maximum(array, -reach), reach).astype(kind)


def setup_inputs(seed: int = 0) -> dict:
    seeds = jax.random.split(jax.random.key(seed), 9)
    return {
        "feats": draw_feats(jax.random.fold_in(seeds[8], 71), 0),
        "w_qkv": bell_draw(seeds[1], (3, D, D), D ** -0.5, 0.375, ((2, 8),)),
        "w_out": bell_draw(seeds[2], (D, D), D ** -0.5, 0.375, ((0, 8),)),
        "virt_embed": bell_draw(seeds[3], (VIRT, D), 1.0, 6.0),
        "member": plant(jax.random.randint(seeds[4], (NODES,), 0, VIRT), jax.random.fold_in(seeds[4], 1), 0, VIRT - 1).astype(jnp.int32),
        "expander": draw_expander(jax.random.fold_in(seeds[8], 71), 0),
        "local_mask": draw_local_mask(jax.random.fold_in(seeds[8], 71), 0),
        "cotangent": bell_draw(seeds[7], (NODES, D), 1.0, 6.0, ((0, 32),)),
    }


masked_score = -1.0e30


def attend_forward(query, keys, values, mask, side_keys, side_values, virt_keys, virt_values, scale):
    query32 = query.astype(jnp.float32)
    local_s = jnp.einsum("rhe,jhe->hrj", query32, keys.astype(jnp.float32)) * scale
    local_s = jnp.where(mask[None] > 0, local_s, masked_score)
    side_s = jnp.einsum("rhe,rkhe->hrk", query32, side_keys.astype(jnp.float32)) * scale
    virt_s = jnp.einsum("rhe,vhe->hrv", query32, virt_keys.astype(jnp.float32)) * scale
    highest = jnp.maximum(jnp.maximum(jnp.max(local_s, axis=2), jnp.max(side_s, axis=2)), jnp.max(virt_s, axis=2))[:, :, None]
    local_w = jnp.where(mask[None] > 0, jnp.exp(local_s - highest), 0.0)
    side_w = jnp.exp(side_s - highest)
    virt_w = jnp.exp(virt_s - highest)
    total = jnp.sum(local_w, axis=2, keepdims=True) + jnp.sum(side_w, axis=2, keepdims=True) + jnp.sum(virt_w, axis=2, keepdims=True)
    local_p = local_w / total
    side_p = side_w / total
    virt_p = virt_w / total
    local_b, side_b, virt_b = lax.optimization_barrier((local_p.astype(jnp.bfloat16), side_p.astype(jnp.bfloat16), virt_p.astype(jnp.bfloat16)))
    output = jnp.einsum("hrj,jhe->rhe", local_b.astype(jnp.float32), values.astype(jnp.float32))
    output = output + jnp.einsum("hrk,rkhe->rhe", side_b.astype(jnp.float32), side_values.astype(jnp.float32))
    output = output + jnp.einsum("hrv,vhe->rhe", virt_b.astype(jnp.float32), virt_values.astype(jnp.float32))
    return output.astype(jnp.bfloat16), (local_p, side_p, virt_p)


def attend_backward(query, keys, values, side_keys, side_values, virt_keys, virt_values, weights, grad_output, scale):
    local_p, side_p, virt_p = weights
    local_b, side_b, virt_b = lax.optimization_barrier((local_p.astype(jnp.bfloat16), side_p.astype(jnp.bfloat16), virt_p.astype(jnp.bfloat16)))
    grad32 = grad_output.astype(jnp.float32)
    query32 = query.astype(jnp.float32)
    local_d = jnp.einsum("rhe,jhe->hrj", grad32, values.astype(jnp.float32))
    side_d = jnp.einsum("rhe,rkhe->hrk", grad32, side_values.astype(jnp.float32))
    virt_d = jnp.einsum("rhe,vhe->hrv", grad32, virt_values.astype(jnp.float32))
    centre = jnp.sum(local_p * local_d, axis=2, keepdims=True) + jnp.sum(side_p * side_d, axis=2, keepdims=True) + jnp.sum(virt_p * virt_d, axis=2, keepdims=True)
    local_g, side_g, virt_g = lax.optimization_barrier(((local_p * (local_d - centre)).astype(jnp.bfloat16), (side_p * (side_d - centre)).astype(jnp.bfloat16), (virt_p * (virt_d - centre)).astype(jnp.bfloat16)))
    local_g32 = local_g.astype(jnp.float32)
    side_g32 = side_g.astype(jnp.float32)
    virt_g32 = virt_g.astype(jnp.float32)
    grad_query = jnp.einsum("hrj,jhe->rhe", local_g32, keys.astype(jnp.float32))
    grad_query = grad_query + jnp.einsum("hrk,rkhe->rhe", side_g32, side_keys.astype(jnp.float32))
    grad_query = grad_query + jnp.einsum("hrv,vhe->rhe", virt_g32, virt_keys.astype(jnp.float32))
    grad_query = (scale * grad_query).astype(jnp.bfloat16)
    grad_keys = scale * jnp.einsum("hrj,rhe->jhe", local_g32, query32)
    grad_values = jnp.einsum("hrj,rhe->jhe", local_b.astype(jnp.float32), grad32)
    grad_side_keys = (scale * jnp.einsum("hrk,rhe->rkhe", side_g32, query32)).astype(jnp.bfloat16)
    grad_side_values = jnp.einsum("hrk,rhe->rkhe", side_b.astype(jnp.float32), grad32).astype(jnp.bfloat16)
    grad_virt_keys = scale * jnp.einsum("hrv,rhe->vhe", virt_g32, query32)
    grad_virt_values = jnp.einsum("hrv,rhe->vhe", virt_b.astype(jnp.float32), grad32)
    return grad_query, grad_keys, grad_values, grad_side_keys, grad_side_values, grad_virt_keys, grad_virt_values


def split_heads(table):
    return table.reshape(table.shape[:-1] + (H, HD))


def slabwise(table):
    return table.reshape((SLABS, NDEV) + table.shape[1:])


def reference(feats, w_qkv, w_out, virt_embed, member, expander, local_mask, cotangent):
    scale = HD ** -0.5
    pool_scale = (VIRT / NODES) ** 0.5
    grad_scale = NODES ** -0.5
    projected = jnp.stack([jnp.dot(feats, w_qkv[index], preferred_element_type=jnp.float32) for index in range(3)]).astype(jnp.bfloat16)
    virt_ids = jnp.arange(VIRT, dtype=jnp.int32)
    member_cols = (member[None, :] == virt_ids[:, None]).astype(jnp.bfloat16)
    pooled = jnp.dot(member_cols, feats, preferred_element_type=jnp.float32)
    virt_state = (virt_embed.astype(jnp.float32) + pool_scale * pooled).astype(jnp.bfloat16)
    virt_keys = jnp.dot(virt_state, w_qkv[1], preferred_element_type=jnp.float32).astype(jnp.bfloat16)
    virt_values = jnp.dot(virt_state, w_qkv[2], preferred_element_type=jnp.float32).astype(jnp.bfloat16)
    virt_key_heads = split_heads(virt_keys)
    virt_value_heads = split_heads(virt_values)
    node_ids = jnp.arange(NODES, dtype=jnp.int32)
    branch_ids = jnp.arange(EXP, dtype=jnp.int32)
    inverse = jnp.zeros((NODES, EXP), jnp.int32).at[expander, branch_ids[None, :]].set(jnp.broadcast_to(node_ids[:, None], (NODES, EXP)))
    side_nodes = jnp.concatenate([expander, inverse], axis=1)
    side_keys = projected[1][side_nodes]
    side_values = projected[2][side_nodes]
    inputs = (slabwise(split_heads(projected[0])), slabwise(split_heads(projected[1])), slabwise(split_heads(projected[2])), slabwise(local_mask), slabwise(split_heads(side_keys)), slabwise(split_heads(side_values)))

    def forward_slab(items):
        output, unused = attend_forward(items[0], items[1], items[2], items[3], items[4], items[5], virt_key_heads, virt_value_heads, scale)
        return output

    attended = lax.map(forward_slab, inputs)
    attended_flat = attended.reshape(NODES, D)
    mixed = (feats.astype(jnp.float32) + jnp.dot(attended_flat, w_out, preferred_element_type=jnp.float32)).astype(jnp.bfloat16)
    grad_attended = jnp.dot(cotangent, w_out.T, preferred_element_type=jnp.float32).astype(jnp.bfloat16)
    grad_out = grad_scale * jnp.dot(attended_flat.T, cotangent, preferred_element_type=jnp.float32)

    def backward_slab(items):
        unused, weights = attend_forward(items[0], items[1], items[2], items[3], items[4], items[5], virt_key_heads, virt_value_heads, scale)
        return attend_backward(items[0], items[1], items[2], items[4], items[5], virt_key_heads, virt_value_heads, weights, items[6], scale)

    results = lax.map(backward_slab, inputs + (slabwise(split_heads(grad_attended)),))
    grad_query, grad_keys, grad_values, grad_side_keys, grad_side_values, grad_virt_keys, grad_virt_values = results
    virt_key_grad = jnp.sum(grad_virt_keys, axis=0).reshape(VIRT, D).astype(jnp.bfloat16)
    virt_value_grad = jnp.sum(grad_virt_values, axis=0).reshape(VIRT, D).astype(jnp.bfloat16)
    side_key_grad = grad_side_keys.reshape(NODES, 2 * EXP, D).astype(jnp.float32)
    side_value_grad = grad_side_values.reshape(NODES, 2 * EXP, D).astype(jnp.float32)
    keys_total = grad_keys.reshape(NODES, D)
    values_total = grad_values.reshape(NODES, D)
    for branch in range(EXP):
        keys_total = keys_total.at[expander[:, branch]].add(side_key_grad[:, branch]).at[inverse[:, branch]].add(side_key_grad[:, EXP + branch])
        values_total = values_total.at[expander[:, branch]].add(side_value_grad[:, branch]).at[inverse[:, branch]].add(side_value_grad[:, EXP + branch])
    keys_grad = keys_total.astype(jnp.bfloat16)
    values_grad = values_total.astype(jnp.bfloat16)
    query_grad = grad_query.reshape(NODES, D)
    grad_virtual = jnp.dot(virt_key_grad, w_qkv[1].T, preferred_element_type=jnp.float32) + jnp.dot(virt_value_grad, w_qkv[2].T, preferred_element_type=jnp.float32)
    grad_feats = cotangent.astype(jnp.float32) + jnp.dot(query_grad, w_qkv[0].T, preferred_element_type=jnp.float32)
    grad_feats = grad_feats + jnp.dot(keys_grad, w_qkv[1].T, preferred_element_type=jnp.float32)
    grad_feats = grad_feats + jnp.dot(values_grad, w_qkv[2].T, preferred_element_type=jnp.float32)
    grad_feats = (grad_feats + pool_scale * grad_virtual[member]).astype(jnp.bfloat16)
    grad_qkv = grad_scale * jnp.stack([
        jnp.dot(feats.T, query_grad, preferred_element_type=jnp.float32),
        jnp.dot(feats.T, keys_grad, preferred_element_type=jnp.float32) + jnp.dot(virt_state.T, virt_key_grad, preferred_element_type=jnp.float32),
        jnp.dot(feats.T, values_grad, preferred_element_type=jnp.float32) + jnp.dot(virt_state.T, virt_value_grad, preferred_element_type=jnp.float32)])
    return mixed, grad_feats, grad_qkv, grad_out, grad_virtual
```

```python
import functools

import jax
import jax.numpy as jnp
from jax import lax
from jax.experimental import pallas as pl
from jax.experimental.pallas import tpu as pltpu
from jax.sharding import PartitionSpec as P

HD = 32
VIRT = 64
SLABS = 32
HEADS = 8
ROWS = 1024
WIDTH = 256
NODES = SLABS * ROWS
BLOCK = ROWS // SLABS
SCALE = HD ** (-0.5)
POOL_SCALE = (VIRT / NODES) ** 0.5
GRAD_SCALE = NODES ** (-0.5)
TI = 256
TA = 512
MASKED = -1e30
LOG2E = 1.4426950408889634
SCALE2 = SCALE * LOG2E

f32 = jnp.float32
bf16 = jnp.bfloat16
i32 = jnp.int32


def dot(a, b):
    return jnp.dot(a, b, preferred_element_type=f32)


def dot_nt(a, b):
    return lax.dot_general(a, b, (((1,), (1,)), ((), ())), preferred_element_type=f32)


def iota(shape, dim):
    return lax.broadcasted_iota(i32, shape, dim)


def hot(cond):
    return jnp.where(cond, 1.0, 0.0).astype(bf16)


def split3(x):
    hi = x.astype(bf16)
    rest = x - hi.astype(f32)
    mid = rest.astype(bf16)
    low = (rest - mid.astype(f32)).astype(bf16)
    return hi, mid, low


def dot3(x, one_hot):
    hi, mid, low = split3(x)
    return dot(hi, one_hot) + dot(mid, one_hot) + dot(low, one_hot)


def lane(shape):
    return iota(shape, len(shape) - 1)


def first_virt(slab):
    return 16 * (slab & 3) + 2 * (slab >> 2)


def branch0(shape):
    return (lane(shape) & 32) == 0


def place_rows(table):
    whole = table.astype(i32)
    hi = (whole >> 5).astype(f32).astype(bf16)
    low = (whole & 31).astype(f32).astype(bf16)
    shape = (SLABS, ROWS)
    own = (iota(shape, 1) >> 5) == iota(shape, 0)
    rows = []
    for e in range(2):
        pick = hot(iota((128, ROWS), 0) == 32 * e + (iota((128, ROWS), 1) & 31))
        full = 32.0 * dot(hi, pick) + dot(low, pick)
        rows.append(jnp.sum(jnp.where(own, full, 0.0), axis=0, keepdims=True))
    return rows


def pool_kernel(feats_at, member_at, expander_at, out, feats, member, expander, sems):
    copies = [
        pltpu.make_async_copy(source, target, sems.at[k])
        for k, (source, target) in enumerate(
            ((feats_at, feats), (member_at, member), (expander_at, expander))
        )
    ]
    for copy in copies:
        copy.start()
    copies[2].wait()
    out[...] = jnp.zeros(out.shape, f32)
    shape = (SLABS, ROWS)
    total = jnp.zeros((SLABS, 128), f32)
    for e in range(2):
        target = expander[e : e + 1, :]
        own = (iota(shape, 1) & 31) == ((iota(shape, 0) - e) & 31)
        hi = jnp.where(own, ((target >> 5) & 31).astype(f32), 0.0).astype(bf16)
        low = jnp.where(own, (target & 31).astype(f32), 0.0).astype(bf16)
        slot = hot((iota((ROWS, 128), 0) >> 5) + 32 * e == iota((ROWS, 128), 1))
        total = total + 32.0 * dot(hi, slot) + dot(low, slot)
    out[:, 4, :] = total
    copies[1].wait()
    shape = (VIRT, ROWS)
    order = iota(shape, 0)
    own = hot(member[...] == first_virt(order & 31) + (order >> 5))
    copies[0].wait()
    pooled = dot(own, feats[...])
    out[:, 0, :] = pooled[:32, :128]
    out[:, 1, :] = pooled[:32, 128:]
    out[:, 2, :] = pooled[32:, :128]
    out[:, 3, :] = pooled[32:, 128:]


def project_kernel(
    feats, cotangent, w_qkv, w_out, embed_in,
    table, kv_weights, share, embed, query_t, grad_t, table_t,
):
    embed[...] = embed_in[...]
    w_q, w_k, w_v = w_qkv[0], w_qkv[1], w_qkv[2]
    w_kv4 = jnp.concatenate([w_k, w_k, w_v, w_v], axis=0)
    kv_weights[...] = w_kv4
    share[...] = jnp.concatenate([w_q, w_k, w_v, w_out[...]], axis=0)
    table[...] = dot_nt(feats[...], w_kv4).astype(bf16)
    query_t[...] = dot_nt(w_q, feats[...]).astype(bf16)
    grad_t[...] = dot_nt(w_out[...], cotangent[...]).astype(bf16)
    table_t[...] = dot_nt(jnp.concatenate([w_k, w_v], axis=0), feats[...]).astype(bf16)


def turn_parts(x):
    turned = x.astype(f32).T
    return (
        jnp.concatenate([turned[0:32], turned[64:96]], axis=0),
        jnp.concatenate([turned[32:64], turned[96:128]], axis=0),
    )


def join_parts(parts):
    first, second = parts
    return jnp.concatenate([first[0:32], second[0:32], first[32:64], second[32:64]], axis=0)


def split_places(places):
    at = iota((256, 128), 0)
    found = []
    for place in places:
        whole = place.astype(i32)
        low = whole & 255
        cols = [hot(at == low[:, 128 * c : 128 * c + 128]) for c in range(8)]
        found.append((whole >> 8, jnp.concatenate(cols, axis=1)))
    return found


def gather_rows(found, pair):
    parts = []
    for (high, low_hot), part in zip(found, pair):
        part = part.astype(bf16)
        left = jnp.concatenate([part[:, 256 * k : 256 * k + 256] for k in range(4)], axis=0)
        got = dot(left, low_hot)
        chosen = got[192:256]
        for k in range(3):
            chosen = jnp.where(high == k, got[64 * k : 64 * k + 64], chosen)
        parts.append(chosen)
    return join_parts(parts)


def scatter_rows(found, pair):
    parts = []
    for (high, low_hot), part in zip(found, pair):
        left = jnp.concatenate([jnp.where(high == k, part, 0.0) for k in range(4)], axis=0)
        got = dot_nt(left.astype(bf16), low_hot)
        parts.append(jnp.concatenate([got[64 * k : 64 * k + 64] for k in range(4)], axis=1))
    return join_parts(parts)


def to_slabs(turned):
    return turned.T.astype(bf16).reshape(SLABS, BLOCK, 128)


def rows_kernel(slab, arrived, table, table_t, virt_embed, kv_weights, out, places, state, wide):
    row0, row1 = place_rows(arrived[:, 4, :])
    at = iota((8, ROWS), 0)
    places[...] = jnp.where(at == 0, row0, jnp.where(at == 1, row1, 0.0))
    shape = (8, VIRT)
    pick = hot((iota(shape, 1) == first_virt(slab[0]) + iota(shape, 0)) & (iota(shape, 0) < 2))
    embed = dot(pick, virt_embed[...])
    pooled = jnp.sum(arrived[...], axis=0)
    first = jnp.concatenate([pooled[0:1], pooled[1:2]], axis=1)
    second = jnp.concatenate([pooled[2:3], pooled[3:4]], axis=1)
    at = iota((8, WIDTH), 0)
    pooled = jnp.where(at == 0, first, jnp.where(at == 1, second, 0.0))
    virt_state = embed + POOL_SCALE * pooled
    at = iota((128, WIDTH), 0) - 2 * (slab[0] >> 2)
    whole = jnp.where(at == 0, virt_state[0:1], jnp.where(at == 1, virt_state[1:2], 0.0))
    state[...] = whole.astype(bf16)
    virt_state = jnp.concatenate([virt_state, jnp.zeros((8, WIDTH), f32)], axis=0).astype(bf16)
    virt_rows = dot_nt(virt_state, kv_weights[...]).astype(bf16)
    out[:, 64:80, :] = jnp.broadcast_to(virt_rows[None], (SLABS, 16, 128))
    wide[...] = table[...].astype(f32)
    leave_rows(wide, out)
    out[:, 32:64, :] = to_slabs(gather_rows(split_places((row0, row1)), (table_t[...],) * 2))


def spread_rows(arrived, at, held):
    blocks = [arrived[s, at : at + 32, :].astype(f32) for s in range(SLABS)]
    low_branch = branch0((BLOCK, 128))
    for s in range(SLABS):
        block = jnp.where(low_branch, blocks[s], blocks[(s + 1) % SLABS])
        held[pl.ds(s, BLOCK, stride=SLABS), :] = block
    return held[...]


def leave_rows(held, out):
    low_branch = branch0((BLOCK, 128))
    blocks = [held[pl.ds(s, BLOCK, stride=SLABS), :] for s in range(SLABS)]
    for s in range(SLABS):
        block = jnp.where(low_branch, blocks[s], blocks[(s - 1) % SLABS])
        out[s, 0:32, :] = block.astype(bf16)


def right_tables(table_t):
    key, value = table_t[0:32, :], table_t[32:64, :]
    at = iota((16, ROWS), 0)
    none = jnp.zeros((16, ROWS), bf16)
    less_base = jnp.where(at < 3, -1.0, 0.0).astype(bf16)
    less_centre = jnp.where((at >= 3) & (at < 6), -1.0, 0.0).astype(bf16)
    keys = jnp.concatenate([key, key, key, less_base, none], axis=0)
    values = jnp.concatenate([none, none, none, none, value, less_centre, none], axis=0)
    return keys, values


def left_query(query, parts):
    wide = [part.astype(f32) for part in split3(query.astype(f32) * SCALE2)]
    rest = jnp.zeros((24, query.shape[1]), f32)
    return jnp.concatenate(wide + [parts, rest], axis=0).T.astype(bf16)


def left_grad(grad, parts):
    rest = jnp.zeros((24, grad.shape[1]), f32)
    front = jnp.zeros((64, grad.shape[1]), f32)
    return jnp.concatenate([front, grad.astype(f32), parts, rest], axis=0).T.astype(bf16)


def stack_rows(rows, fill):
    at = iota((8, ROWS), 0)
    block = jnp.full((8, ROWS), fill, f32)
    for k, row in enumerate(rows):
        block = jnp.where(at == k, row, block)
    return block


def local_kernel(query_t, grad_t, mask, table_t, stats):
    none = jnp.zeros((8, TI), f32)
    q_own = left_query(query_t[...], none)
    g_own = left_grad(grad_t[...], none)
    keys, values = right_tables(table_t)
    scores = jnp.where(mask[...] > 0, dot(q_own, keys), MASKED)
    highest = jnp.max(scores, axis=1, keepdims=True)
    weight = jnp.exp2(scores - highest)
    value_dots = dot(g_own, values)
    total = jnp.sum(weight, axis=1, keepdims=True)
    centre = jnp.sum(weight * value_dots, axis=1, keepdims=True)
    at = lane((TI, 128))
    stat = jnp.where(at == 0, highest, jnp.where(at == 1, total, centre))
    stats[...] = stat.T[0:8]


def side_kernel(
    query_t, grad_t, stats, arrived, places,
    out, parts_out, attended_out, grad_query_out,
    near,
):
    virt_rows = arrived[:, 64:80, :].astype(f32)
    pieces = [virt_rows[4 * ((v & 15) >> 1) + (v >> 4), 0:2, :] for v in range(0, VIRT, 2)]
    virt_rows = jnp.concatenate(pieces, axis=0)
    at = lane((VIRT, 128))
    virt_left = jnp.where(at < 64, virt_rows, 0.0), jnp.where(at >= 64, virt_rows, 0.0)
    virt_left = jnp.concatenate(virt_left, axis=0).astype(bf16)
    virt_t = jnp.concatenate([virt_rows, jnp.zeros((64, 128), f32)], axis=0).T.astype(bf16)
    found = split_places((places[0:1, :], places[1:2, :]))
    forward = spread_rows(arrived, 32, near).T
    inverse = scatter_rows(found, turn_parts(arrived[:, 0:32, :].reshape(ROWS, 128)))
    side_k = (forward[0:32], forward[32:64], inverse[0:32], inverse[32:64])
    side_v = (forward[64:96], forward[96:128], inverse[64:96], inverse[96:128])
    q_t, g_t = query_t[...], grad_t[...]
    q_wide, g_wide = q_t.astype(f32), g_t.astype(f32)
    none = jnp.zeros((32, ROWS), bf16)
    virt = dot(virt_left, jnp.concatenate([q_t, none, g_t, none], axis=0))
    virt_s, virt_d = SCALE2 * virt[0:VIRT], virt[VIRT:]
    side_s = [SCALE2 * jnp.sum(q_wide * part, axis=0, keepdims=True) for part in side_k]
    side_d = [jnp.sum(g_wide * part, axis=0, keepdims=True) for part in side_v]
    side_s, side_d = stack_rows(side_s, MASKED), stack_rows(side_d, 0.0)
    local_m, local_t, local_c = stats[0:1, :], stats[1:2, :], stats[2:3, :]
    highest = jnp.maximum(jnp.max(virt_s, axis=0, keepdims=True), jnp.max(side_s, axis=0, keepdims=True))
    highest = jnp.maximum(local_m, highest)
    virt_p = jnp.exp2(virt_s - highest)
    side_p = jnp.exp2(side_s - highest)
    factor = jnp.exp2(local_m - highest)
    total = factor * local_t
    total = total + jnp.sum(virt_p, axis=0, keepdims=True) + jnp.sum(side_p, axis=0, keepdims=True)
    share = 1.0 / total
    virt_p = virt_p * share
    side_p = side_p * share
    centre = factor * share * local_c + jnp.sum(virt_p * virt_d, axis=0, keepdims=True)
    centre = centre + jnp.sum(side_p * side_d, axis=0, keepdims=True)
    base = highest + LOG2E * jnp.log(total)
    parts = [part.astype(f32) for column in (base, centre) for part in split3(column)]
    parts_out[...] = stack_rows(parts, 0.0)
    virt_g = (virt_p * (virt_d - centre)).astype(bf16)
    virt_p = virt_p.astype(bf16)
    side_g = (side_p * (side_d - centre)).astype(bf16).astype(f32)
    side_p = side_p.astype(bf16).astype(f32)
    attended = dot(virt_t[64:96, 0:VIRT], virt_p)
    grad_query = dot(virt_t[0:32, 0:VIRT], virt_g)
    key_terms, value_terms = [], []
    for k in range(4):
        one_p, one_g = side_p[k : k + 1], side_g[k : k + 1]
        attended = attended + one_p * side_v[k]
        grad_query = grad_query + one_g * side_k[k]
        key_terms.append((SCALE * (one_g * q_wide)).astype(bf16).astype(f32))
        value_terms.append((one_p * g_wide).astype(bf16).astype(f32))
    near[...] = jnp.concatenate(key_terms[:2] + value_terms[:2], axis=0).T
    leave_rows(near, out)
    pair = [jnp.concatenate([key_terms[k], value_terms[k]], axis=0) for k in (2, 3)]
    out[:, 32:64, :] = to_slabs(gather_rows(found, pair))
    sums = jnp.concatenate([SCALE * dot_nt(q_t, virt_g), dot_nt(g_t, virt_p)], axis=0)
    hi = sums.astype(bf16).astype(f32)
    both_parts = jnp.concatenate([hi, sums - hi], axis=0)
    both_parts = jnp.concatenate([both_parts, jnp.zeros((128, 64), f32)], axis=1).T[0:VIRT]
    both_parts = both_parts.astype(bf16)
    for slab in range(SLABS):
        first = 16 * (slab & 3)
        out[slab, 64:80, :] = both_parts[first : first + 16]
    attended_out[...] = attended
    grad_query_out[...] = grad_query


def attend_kernel(
    parts, attended, grad_query, query_t, grad_t, table_t, cotangent_at, mask_at,
    local, result, out_term,
    cotangent, mask, sems,
):
    tiles = ROWS // TA
    copies = []
    for tile in range(tiles):
        span = pl.ds(tile * TA, TA)
        copies.append(pltpu.make_async_copy(mask_at.at[span], mask.at[span], sems.at[tile]))
    copies.append(pltpu.make_async_copy(cotangent_at, cotangent, sems.at[tiles]))
    for copy in copies:
        copy.start()
    all_keys, all_values = right_tables(table_t)
    q_t, g_t = query_t[...], grad_t[...]
    q_own = left_query(q_t, parts[...])
    g_own = left_grad(g_t, parts[...])
    key_t, value_t = table_t[0:32, :], table_t[32:64, :]
    grad_k = jnp.zeros((32, ROWS), f32)
    grad_v = jnp.zeros((32, ROWS), f32)
    for tile in range(tiles):
        span = slice(tile * TA, tile * TA + TA)
        copies[tile].wait()
        scores = jnp.where(mask[span, :] > 0, dot(q_own[span], all_keys), MASKED)
        weight = jnp.exp2(scores)
        local_p = weight.astype(bf16)
        local_g = (weight * dot(g_own[span], all_values)).astype(bf16)
        result[0:32, span] = (SCALE * (grad_query[:, span] + dot_nt(key_t, local_g))).astype(bf16)
        result[32:64, span] = (attended[:, span] + dot_nt(value_t, local_p)).astype(bf16)
        grad_k = grad_k + dot(q_t[:, span], local_g)
        grad_v = grad_v + dot(g_t[:, span], local_p)
    local[0:32, :] = SCALE * grad_k
    local[32:64, :] = grad_v
    copies[tiles].wait()
    out_term[...] = GRAD_SCALE * dot(result[32:64, :], cotangent[...])


def gather_kernel(arrived, places, local, result, rows_out, stacked_out, virt_out, near):
    found = split_places((places[0:1, :], places[1:2, :]))
    forward = scatter_rows(found, turn_parts(arrived[:, 0:32, :].reshape(ROWS, 128)))
    side = forward + spread_rows(arrived, 32, near).T
    keys_grad = (local[0:32, :] + side[0:32] + side[32:64]).astype(bf16)
    values_grad = (local[32:64, :] + side[64:96] + side[96:128]).astype(bf16)
    stacked = jnp.concatenate([result[0:32, :], keys_grad, values_grad, result[32:64, :]], axis=0)
    stacked_out[...] = stacked
    rows_out[:, 0:128, :] = stacked.astype(f32).T.astype(bf16).reshape(HEADS, 128, 128)
    parts = jnp.sum(arrived[:, 64:80, :].astype(f32), axis=0)
    virt = (parts + pltpu.roll(parts, 64, 1)).astype(bf16).astype(f32)
    inner = (lane((16, 128)) >= 32) & (lane((16, 128)) < 96)
    virt = jnp.where(inner, pltpu.roll(virt, 32, 1), 0.0)
    virt_out[...] = virt
    rows_out[:, 128:144, :] = jnp.broadcast_to(virt.astype(bf16)[None], (HEADS, 16, 128))


def partial_kernel(core, stacked, virt, feats, state, out_term, keep, give, held):
    virt = jnp.concatenate([virt[...], jnp.zeros((112, 128), f32)], axis=0)
    grads = dot(stacked[...], feats[...]) + dot(virt.T.astype(bf16), state[...])
    held[0] = GRAD_SCALE * grads[0:64]
    held[1, 0:32, :] = GRAD_SCALE * grads[64:96]
    held[1, 32:64, :] = out_term[...]
    keep[...] = held[core[0]]
    give[...] = held[1 - core[0]]


def mix_kernel(
    head, group, rows, weights0, weights1, weights2, weights3, feats_at, cotangent_at,
    columns, virt_out, feats, cotangent, turned, sems,
):
    which = head[0]
    span = pl.ds(pl.multiple_of(which * 128, 128), 128)
    copies = [
        pltpu.make_async_copy(feats_at.at[span], feats, sems.at[0]),
        pltpu.make_async_copy(cotangent_at.at[span], cotangent, sems.at[1]),
    ]
    for copy in copies:
        copy.start()
    grads = jnp.zeros((144, WIDTH), f32)
    mixed = jnp.zeros((128, WIDTH), f32)
    inner = lane((144, 128)) < 96
    for turn in (0, 4, 1, 5, 2, 6, 7, 3):
        row = rows[(which + turn) & 7]
        zero = jnp.zeros_like(row)
        source = (weights0, weights1, weights2, weights3)[turn & 3]
        at = 128 if turn in (3, 4, 5, 6) else 0
        weight = source[at : at + 128, :]
        grads = grads + dot(jnp.where(inner, row, zero), weight)
        mixed = mixed + dot(jnp.where(inner, zero, row)[0:128], weight)
    turned[...] = jnp.concatenate([grads[128:144], jnp.zeros((112, WIDTH), f32)], axis=0).T
    own = turned[pl.ds(pl.multiple_of(which * 32, 32), 32), :]
    virt_out[...] = pltpu.roll(own, 16 * group[0], 1)
    for copy in copies:
        copy.wait()
    grads = (cotangent[...].astype(f32) + grads[0:128]).T
    mixed = (feats[...].astype(f32) + mixed).T.astype(bf16)
    hi = grads.astype(bf16)
    low = (grads - hi.astype(f32)).astype(bf16)
    columns[:, 0:32, :] = mixed.reshape(HEADS, 32, 128)
    columns[:, 32:64, :] = hi.reshape(HEADS, 32, 128)
    columns[:, 64:96, :] = low.reshape(HEADS, 32, 128)


def finish_kernel(
    core, columns, near, far, virt0, virt1, virt2, virt3, member,
    mixed, grad_feats, grad_qkv, grad_out, grad_virtual, held,
):
    held[core[0]] = near[...]
    held[1 - core[0]] = far[...]
    grad_qkv[0:64, :] = held[0]
    grad_qkv[64:96, :] = held[1, 0:32, :]
    grad_out[...] = held[1, 32:64, :]
    virt = (virt0[...] + virt1[...]) + (virt2[...] + virt3[...])
    grad_virtual[...] = virt[:, :VIRT]
    lookup = POOL_SCALE * dot3(virt, hot(member[...] == iota((128, ROWS), 0)))
    for h in range(HEADS):
        at = slice(128 * h, 128 * h + 128)
        mixed[:, at] = columns[h, 0:32, :]
        whole = columns[h, 32:64, :].astype(f32) + columns[h, 64:96, :].astype(f32)
        grad_feats[:, at] = (whole + lookup[:, at]).astype(bf16)


def array(shape, kind):
    return jax.ShapeDtypeStruct(shape, kind)


VMEM = pl.BlockSpec(memory_space=pltpu.VMEM)
SMEM = pl.BlockSpec(memory_space=pltpu.SMEM)
HBM = pl.BlockSpec(memory_space=pltpu.HBM)


def call(kernel, specs, outs, scratch=(), mib=48, **named):
    return pl.pallas_call(
        kernel,
        out_shape=outs,
        in_specs=specs,
        out_specs=jax.tree.map(lambda _: VMEM, outs),
        scratch_shapes=list(scratch),
        compiler_params=pltpu.CompilerParams(vmem_limit_bytes=mib * 1024 * 1024),
        **named,
    )


def exchange(x, axis):
    return lax.all_to_all(x, axis, split_axis=0, concat_axis=0, tiled=True)


def swap(x, axis, k):
    return lax.ppermute(x, axis, [(i, i ^ k) for i in range(lax.axis_size(axis))])


def shift(x, k):
    return lax.ppermute(x, "head", [((h + k) % HEADS, h) for h in range(HEADS)])


def shards(feats, w_qkv, w_out, virt_embed, member, expander, local_mask, cotangent):
    slab = lax.axis_index("dom").astype(i32).reshape(1)
    head = lax.axis_index("head").astype(i32).reshape(1)
    members = member.reshape(1, ROWS)
    first = call(
        pool_kernel,
        [HBM] * 3,
        array((SLABS, 8, 128), f32),
        scratch=[
            pltpu.VMEM((ROWS, WIDTH), bf16),
            pltpu.VMEM((1, ROWS), i32),
            pltpu.VMEM((2, ROWS), i32),
            pltpu.SemaphoreType.DMA((3,)),
        ],
        mib=60,
    )(feats, members, expander.T)
    feats_late, first = lax.optimization_barrier([feats, first])
    first = exchange(first, "dom")
    table, kv_weights, share, embed, query_t, grad_t, table_t = call(
        project_kernel,
        [VMEM] * 5,
        (
            array((ROWS, 128), bf16),
            array((128, WIDTH), bf16),
            array((128, WIDTH), bf16),
            array((VIRT, WIDTH), bf16),
            array((32, ROWS), bf16),
            array((32, ROWS), bf16),
            array((64, ROWS), bf16),
        ),
    )(feats_late, cotangent, jnp.transpose(w_qkv, (0, 2, 1)), w_out, virt_embed)
    second, places, state = call(
        rows_kernel,
        [SMEM] + [VMEM] * 5,
        (array((SLABS, 80, 128), bf16), array((8, ROWS), f32), array((128, WIDTH), bf16)),
        scratch=[pltpu.VMEM((ROWS, 128), f32)],
    )(slab, first, table, table_t, embed, kv_weights)
    second, share, query_t = lax.optimization_barrier([second, share, query_t])
    two = jnp.concatenate([share, swap(share, "head", 4)], axis=0)
    across = lambda rows: pl.BlockSpec((rows, TI), lambda i: (0, i))
    stats = pl.pallas_call(
        local_kernel,
        grid=(ROWS // TI,),
        out_shape=array((8, ROWS), f32),
        in_specs=[across(32), across(32), pl.BlockSpec((TI, ROWS), lambda i: (i, 0)), VMEM],
        out_specs=across(8),
        compiler_params=pltpu.CompilerParams(vmem_limit_bytes=48 * 1024 * 1024),
    )(query_t, grad_t, local_mask, table_t)
    second, two, stats = lax.optimization_barrier([exchange(second, "dom"), two, stats])
    third, parts, attended, grad_query = call(
        side_kernel,
        [VMEM] * 5,
        (
            array((SLABS, 80, 128), bf16),
            array((8, ROWS), f32),
            array((32, ROWS), f32),
            array((32, ROWS), f32),
        ),
        scratch=[pltpu.VMEM((ROWS, 128), f32)],
    )(query_t, grad_t, stats, second, places)
    local, result, out_term = call(
        attend_kernel,
        [VMEM] * 6 + [HBM] * 2,
        (array((64, ROWS), f32), array((64, ROWS), bf16), array((32, WIDTH), f32)),
        scratch=[
            pltpu.VMEM((ROWS, WIDTH), bf16),
            pltpu.VMEM((ROWS, ROWS), i32),
            pltpu.SemaphoreType.DMA((ROWS // TA + 1,)),
        ],
    )(parts, attended, grad_query, query_t, grad_t, table_t, cotangent, local_mask)
    third, two = lax.optimization_barrier([third, two])
    others = [shift(two, k) for k in (1, 2, 7)]
    third, *others = lax.optimization_barrier([exchange(third, "dom")] + others)
    rows, stacked, virt = call(
        gather_kernel,
        [VMEM] * 4,
        (array((HEADS, 144, 128), bf16), array((128, ROWS), bf16), array((16, 128), f32)),
        scratch=[
            pltpu.VMEM((ROWS, 128), f32),
        ],
    )(third, places, local, result)
    rows, stacked = lax.optimization_barrier([rows, stacked])
    rows = exchange(rows, "head")
    keep, give = call(
        partial_kernel,
        [SMEM] + [VMEM] * 5,
        (array((64, WIDTH), f32), array((64, WIDTH), f32)),
        scratch=[pltpu.VMEM((2, 64, WIDTH), f32)],
    )(slab & 1, stacked, virt, feats, state, out_term)
    keep = keep + swap(give, "dom", 1)
    keep = (keep + swap(keep, "dom", 2)) + (swap(keep, "dom", 4) + swap(keep, "dom", 6))
    rows, keep = lax.optimization_barrier([rows, keep])
    columns, virt = call(
        mix_kernel,
        [SMEM] * 2 + [VMEM] * 5 + [HBM] * 2,
        (array((HEADS, 96, 128), bf16), array((32, 128), f32)),
        scratch=[
            pltpu.VMEM((128, WIDTH), bf16),
            pltpu.VMEM((128, WIDTH), bf16),
            pltpu.VMEM((WIDTH, 128), f32),
            pltpu.SemaphoreType.DMA((2,)),
        ],
    )(head, slab & 3, rows, two, *others, feats, cotangent)
    columns = exchange(columns, "head")
    keep = (keep + swap(keep, "dom", 8)) + (swap(keep, "dom", 16) + swap(keep, "dom", 24))
    virts = [virt] + [swap(virt, "dom", k) for k in (1, 2, 3)]
    mixed, grad_feats, grad_qkv, grad_out, grad_virtual = call(
        finish_kernel,
        [SMEM] + [VMEM] * 8,
        (
            array((32, ROWS), bf16),
            array((32, ROWS), bf16),
            array((96, WIDTH), f32),
            array((32, WIDTH), f32),
            array((32, VIRT), f32),
        ),
        scratch=[pltpu.VMEM((2, 64, WIDTH), f32)],
    )(slab & 1, columns, keep, swap(keep, "dom", 1), *virts, members)
    grad_qkv = jnp.transpose(grad_qkv.reshape(3, 32, WIDTH), (0, 2, 1))
    return (mixed.T, grad_feats.T, grad_qkv, grad_out, grad_virtual.T)


def solution(mesh):
    return jax.shard_map(
        shards,
        mesh=mesh,
        in_specs=(
            P("dom", None),
            P(None, None, "head"),
            P("head", None),
            P(),
            P("dom"),
            P("dom", None),
            P("dom", None),
            P("dom", None),
        ),
        out_specs=(
            P("dom", "head"),
            P("dom", "head"),
            P(None, None, "head"),
            P("head", None),
            P(None, "head"),
        ),
        check_vma=False,
    )
```

```python
import functools

import jax
import jax.numpy as jnp
from jax import lax
from jax.experimental import pallas as pl
from jax.experimental.pallas import tpu as pltpu
from jax.sharding import PartitionSpec as P

HD = 32
VIRT = 64
SLABS = 32
HEADS = 8
ROWS = 1024
WIDTH = 256
NODES = SLABS * ROWS
BLOCK = ROWS // SLABS
SCALE = HD ** (-0.5)
POOL_SCALE = (VIRT / NODES) ** 0.5
GRAD_SCALE = NODES ** (-0.5)
TI = 256
TA = 512
MASKED = -1e30
LOG2E = 1.4426950408889634
SCALE2 = SCALE * LOG2E

f32 = jnp.float32
bf16 = jnp.bfloat16
i32 = jnp.int32


def dot(a, b):
    return jnp.dot(a, b, preferred_element_type=f32)


def dot_nt(a, b):
    return lax.dot_general(a, b, (((1,), (1,)), ((), ())), preferred_element_type=f32)


def iota(shape, dim):
    return lax.broadcasted_iota(i32, shape, dim)


def hot(cond):
    return jnp.where(cond, 1.0, 0.0).astype(bf16)


def split3(x):
    hi = x.astype(bf16)
    rest = x - hi.astype(f32)
    mid = rest.astype(bf16)
    low = (rest - mid.astype(f32)).astype(bf16)
    return hi, mid, low


def dot3(x, one_hot):
    hi, mid, low = split3(x)
    return dot(hi, one_hot) + dot(mid, one_hot) + dot(low, one_hot)


def lane(shape):
    return iota(shape, len(shape) - 1)


def first_virt(slab):
    return 16 * (slab & 3) + 2 * (slab >> 2)


def branch0(shape):
    return (lane(shape) & 32) == 0


def place_rows(table):
    whole = table.astype(i32)
    hi = (whole >> 5).astype(f32).astype(bf16)
    low = (whole & 31).astype(f32).astype(bf16)
    shape = (SLABS, ROWS)
    own = (iota(shape, 1) >> 5) == iota(shape, 0)
    rows = []
    for e in range(2):
        pick = hot(iota((128, ROWS), 0) == 32 * e + (iota((128, ROWS), 1) & 31))
        full = 32.0 * dot(hi, pick) + dot(low, pick)
        rows.append(jnp.sum(jnp.where(own, full, 0.0), axis=0, keepdims=True))
    return rows


def pool_kernel(feats_at, member_at, expander_at, out, feats, member, expander, sems):
    copies = [
        pltpu.make_async_copy(source, target, sems.at[k])
        for k, (source, target) in enumerate(
            ((feats_at, feats), (member_at, member), (expander_at, expander))
        )
    ]
    for copy in copies:
        copy.start()
    copies[2].wait()
    out[...] = jnp.zeros(out.shape, f32)
    shape = (SLABS, ROWS)
    total = jnp.zeros((SLABS, 128), f32)
    for e in range(2):
        target = expander[e : e + 1, :]
        own = (iota(shape, 1) & 31) == ((iota(shape, 0) - e) & 31)
        hi = jnp.where(own, ((target >> 5) & 31).astype(f32), 0.0).astype(bf16)
        low = jnp.where(own, (target & 31).astype(f32), 0.0).astype(bf16)
        slot = hot((iota((ROWS, 128), 0) >> 5) + 32 * e == iota((ROWS, 128), 1))
        total = total + 32.0 * dot(hi, slot) + dot(low, slot)
    out[:, 4, :] = total
    copies[1].wait()
    shape = (VIRT, ROWS)
    order = iota(shape, 0)
    own = hot(member[...] == first_virt(order & 31) + (order >> 5))
    copies[0].wait()
    pooled = dot(own, feats[...])
    out[:, 0, :] = pooled[:32, :128]
    out[:, 1, :] = pooled[:32, 128:]
    out[:, 2, :] = pooled[32:, :128]
    out[:, 3, :] = pooled[32:, 128:]


def project_kernel(
    feats, cotangent, w_qkv, w_out, embed_in,
    table, kv_weights, share, embed, query_t, grad_t, table_t,
):
    embed[...] = embed_in[...]
    w_q, w_k, w_v = w_qkv[0], w_qkv[1], w_qkv[2]
    w_kv4 = jnp.concatenate([w_k, w_k, w_v, w_v], axis=0)
    kv_weights[...] = w_kv4
    share[...] = jnp.concatenate([w_q, w_k, w_v, w_out[...]], axis=0)
    table[...] = dot_nt(feats[...], w_kv4).astype(bf16)
    query_t[...] = dot_nt(w_q, feats[...]).astype(bf16)
    grad_t[...] = dot_nt(w_out[...], cotangent[...]).astype(bf16)
    table_t[...] = dot_nt(jnp.concatenate([w_k, w_v], axis=0), feats[...]).astype(bf16)


def turn_parts(x):
    turned = x.astype(f32).T
    return (
        jnp.concatenate([turned[0:32], turned[64:96]], axis=0),
        jnp.concatenate([turned[32:64], turned[96:128]], axis=0),
    )


def join_parts(parts):
    first, second = parts
    return jnp.concatenate([first[0:32], second[0:32], first[32:64], second[32:64]], axis=0)


def split_places(places):
    at = iota((256, 128), 0)
    found = []
    for place in places:
        whole = place.astype(i32)
        low = whole & 255
        cols = [hot(at == low[:, 128 * c : 128 * c + 128]) for c in range(8)]
        found.append((whole >> 8, jnp.concatenate(cols, axis=1)))
    return found


def gather_rows(found, pair):
    parts = []
    for (high, low_hot), part in zip(found, pair):
        part = part.astype(bf16)
        left = jnp.concatenate([part[:, 256 * k : 256 * k + 256] for k in range(4)], axis=0)
        got = dot(left, low_hot)
        chosen = got[192:256]
        for k in range(3):
            chosen = jnp.where(high == k, got[64 * k : 64 * k + 64], chosen)
        parts.append(chosen)
    return join_parts(parts)


def scatter_rows(found, pair):
    parts = []
    for (high, low_hot), part in zip(found, pair):
        left = jnp.concatenate([jnp.where(high == k, part, 0.0) for k in range(4)], axis=0)
        got = dot_nt(left.astype(bf16), low_hot)
        parts.append(jnp.concatenate([got[64 * k : 64 * k + 64] for k in range(4)], axis=1))
    return join_parts(parts)


def to_slabs(turned):
    return turned.T.astype(bf16).reshape(SLABS, BLOCK, 128)


def rows_kernel(slab, arrived, table, table_t, virt_embed, kv_weights, out, places, state, wide):
    row0, row1 = place_rows(arrived[:, 4, :])
    at = iota((8, ROWS), 0)
    places[...] = jnp.where(at == 0, row0, jnp.where(at == 1, row1, 0.0))
    shape = (8, VIRT)
    pick = hot((iota(shape, 1) == first_virt(slab[0]) + iota(shape, 0)) & (iota(shape, 0) < 2))
    embed = dot(pick, virt_embed[...])
    pooled = jnp.sum(arrived[...], axis=0)
    first = jnp.concatenate([pooled[0:1], pooled[1:2]], axis=1)
    second = jnp.concatenate([pooled[2:3], pooled[3:4]], axis=1)
    at = iota((8, WIDTH), 0)
    pooled = jnp.where(at == 0, first, jnp.where(at == 1, second, 0.0))
    virt_state = embed + POOL_SCALE * pooled
    at = iota((128, WIDTH), 0) - 2 * (slab[0] >> 2)
    whole = jnp.where(at == 0, virt_state[0:1], jnp.where(at == 1, virt_state[1:2], 0.0))
    state[...] = whole.astype(bf16)
    virt_state = jnp.concatenate([virt_state, jnp.zeros((8, WIDTH), f32)], axis=0).astype(bf16)
    virt_rows = dot_nt(virt_state, kv_weights[...]).astype(bf16)
    out[:, 64:80, :] = jnp.broadcast_to(virt_rows[None], (SLABS, 16, 128))
    wide[...] = table[...].astype(f32)
    leave_rows(wide, out)
    out[:, 32:64, :] = to_slabs(gather_rows(split_places((row0, row1)), (table_t[...],) * 2))


def spread_rows(arrived, at, held):
    blocks = [arrived[s, at : at + 32, :].astype(f32) for s in range(SLABS)]
    low_branch = branch0((BLOCK, 128))
    for s in range(SLABS):
        block = jnp.where(low_branch, blocks[s], blocks[(s + 1) % SLABS])
        held[pl.ds(s, BLOCK, stride=SLABS), :] = block
    return held[...]


def leave_rows(held, out):
    low_branch = branch0((BLOCK, 128))
    blocks = [held[pl.ds(s, BLOCK, stride=SLABS), :] for s in range(SLABS)]
    for s in range(SLABS):
        block = jnp.where(low_branch, blocks[s], blocks[(s - 1) % SLABS])
        out[s, 0:32, :] = block.astype(bf16)


def right_tables(table_t):
    key, value = table_t[0:32, :], table_t[32:64, :]
    at = iota((16, ROWS), 0)
    none = jnp.zeros((16, ROWS), bf16)
    less_base = jnp.where(at < 3, -1.0, 0.0).astype(bf16)
    less_centre = jnp.where((at >= 3) & (at < 6), -1.0, 0.0).astype(bf16)
    keys = jnp.concatenate([key, key, key, less_base, none], axis=0)
    values = jnp.concatenate([none, none, none, none, value, less_centre, none], axis=0)
    return keys, values


def left_query(query, parts):
    wide = [part.astype(f32) for part in split3(query.astype(f32) * SCALE2)]
    rest = jnp.zeros((24, query.shape[1]), f32)
    return jnp.concatenate(wide + [parts, rest], axis=0).T.astype(bf16)


def left_grad(grad, parts):
    rest = jnp.zeros((24, grad.shape[1]), f32)
    front = jnp.zeros((64, grad.shape[1]), f32)
    return jnp.concatenate([front, grad.astype(f32), parts, rest], axis=0).T.astype(bf16)


def stack_rows(rows, fill):
    at = iota((8, ROWS), 0)
    block = jnp.full((8, ROWS), fill, f32)
    for k, row in enumerate(rows):
        block = jnp.where(at == k, row, block)
    return block


def local_kernel(query_t, grad_t, mask, table_t, stats):
    none = jnp.zeros((8, TI), f32)
    q_own = left_query(query_t[...], none)
    g_own = left_grad(grad_t[...], none)
    keys, values = right_tables(table_t)
    scores = jnp.where(mask[...] > 0, dot(q_own, keys), MASKED)
    highest = jnp.max(scores, axis=1, keepdims=True)
    weight = jnp.exp2(scores - highest)
    value_dots = dot(g_own, values)
    total = jnp.sum(weight, axis=1, keepdims=True)
    centre = jnp.sum(weight * value_dots, axis=1, keepdims=True)
    at = lane((TI, 128))
    stat = jnp.where(at == 0, highest, jnp.where(at == 1, total, centre))
    stats[...] = stat.T[0:8]


def side_kernel(
    query_t, grad_t, stats, arrived, places,
    out, parts_out, attended_out, grad_query_out,
    near,
):
    virt_rows = arrived[:, 64:80, :].astype(f32)
    pieces = [virt_rows[4 * ((v & 15) >> 1) + (v >> 4), 0:2, :] for v in range(0, VIRT, 2)]
    virt_rows = jnp.concatenate(pieces, axis=0)
    at = lane((VIRT, 128))
    virt_left = jnp.where(at < 64, virt_rows, 0.0), jnp.where(at >= 64, virt_rows, 0.0)
    virt_left = jnp.concatenate(virt_left, axis=0).astype(bf16)
    virt_t = jnp.concatenate([virt_rows, jnp.zeros((64, 128), f32)], axis=0).T.astype(bf16)
    found = split_places((places[0:1, :], places[1:2, :]))
    forward = spread_rows(arrived, 32, near).T
    inverse = scatter_rows(found, turn_parts(arrived[:, 0:32, :].reshape(ROWS, 128)))
    side_k = (forward[0:32], forward[32:64], inverse[0:32], inverse[32:64])
    side_v = (forward[64:96], forward[96:128], inverse[64:96], inverse[96:128])
    q_t, g_t = query_t[...], grad_t[...]
    q_wide, g_wide = q_t.astype(f32), g_t.astype(f32)
    none = jnp.zeros((32, ROWS), bf16)
    virt = dot(virt_left, jnp.concatenate([q_t, none, g_t, none], axis=0))
    virt_s, virt_d = SCALE2 * virt[0:VIRT], virt[VIRT:]
    side_s = [SCALE2 * jnp.sum(q_wide * part, axis=0, keepdims=True) for part in side_k]
    side_d = [jnp.sum(g_wide * part, axis=0, keepdims=True) for part in side_v]
    side_s, side_d = stack_rows(side_s, MASKED), stack_rows(side_d, 0.0)
    local_m, local_t, local_c = stats[0:1, :], stats[1:2, :], stats[2:3, :]
    highest = jnp.maximum(jnp.max(virt_s, axis=0, keepdims=True), jnp.max(side_s, axis=0, keepdims=True))
    highest = jnp.maximum(local_m, highest)
    virt_p = jnp.exp2(virt_s - highest)
    side_p = jnp.exp2(side_s - highest)
    factor = jnp.exp2(local_m - highest)
    total = factor * local_t
    total = total + jnp.sum(virt_p, axis=0, keepdims=True) + jnp.sum(side_p, axis=0, keepdims=True)
    share = 1.0 / total
    virt_p = virt_p * share
    side_p = side_p * share
    centre = factor * share * local_c + jnp.sum(virt_p * virt_d, axis=0, keepdims=True)
    centre = centre + jnp.sum(side_p * side_d, axis=0, keepdims=True)
    base = highest + LOG2E * jnp.log(total)
    parts = [part.astype(f32) for column in (base, centre) for part in split3(column)]
    parts_out[...] = stack_rows(parts, 0.0)
    virt_g = (virt_p * (virt_d - centre)).astype(bf16)
    virt_p = virt_p.astype(bf16)
    side_g = (side_p * (side_d - centre)).astype(bf16).astype(f32)
    side_p = side_p.astype(bf16).astype(f32)
    attended = dot(virt_t[64:96, 0:VIRT], virt_p)
    grad_query = dot(virt_t[0:32, 0:VIRT], virt_g)
    key_terms, value_terms = [], []
    for k in range(4):
        one_p, one_g = side_p[k : k + 1], side_g[k : k + 1]
        attended = attended + one_p * side_v[k]
        grad_query = grad_query + one_g * side_k[k]
        key_terms.append((SCALE * (one_g * q_wide)).astype(bf16).astype(f32))
        value_terms.append((one_p * g_wide).astype(bf16).astype(f32))
    near[...] = jnp.concatenate(key_terms[:2] + value_terms[:2], axis=0).T
    leave_rows(near, out)
    pair = [jnp.concatenate([key_terms[k], value_terms[k]], axis=0) for k in (2, 3)]
    out[:, 32:64, :] = to_slabs(gather_rows(found, pair))
    sums = jnp.concatenate([SCALE * dot_nt(q_t, virt_g), dot_nt(g_t, virt_p)], axis=0)
    hi = sums.astype(bf16).astype(f32)
    both_parts = jnp.concatenate([hi, sums - hi], axis=0)
    both_parts = jnp.concatenate([both_parts, jnp.zeros((128, 64), f32)], axis=1).T[0:VIRT]
    both_parts = both_parts.astype(bf16)
    for slab in range(SLABS):
        first = 16 * (slab & 3)
        out[slab, 64:80, :] = both_parts[first : first + 16]
    attended_out[...] = attended
    grad_query_out[...] = grad_query


def attend_kernel(
    parts, attended, grad_query, query_t, grad_t, table_t, cotangent_at, mask_at,
    local, result, out_term,
    cotangent, mask, sems,
):
    tiles = ROWS // TA
    copies = []
    for tile in range(tiles):
        span = pl.ds(tile * TA, TA)
        copies.append(pltpu.make_async_copy(mask_at.at[span], mask.at[span], sems.at[tile]))
    copies.append(pltpu.make_async_copy(cotangent_at, cotangent, sems.at[tiles]))
    for copy in copies:
        copy.start()
    all_keys, all_values = right_tables(table_t)
    q_t, g_t = query_t[...], grad_t[...]
    q_own = left_query(q_t, parts[...])
    g_own = left_grad(g_t, parts[...])
    key_t, value_t = table_t[0:32, :], table_t[32:64, :]
    grad_k = jnp.zeros((32, ROWS), f32)
    grad_v = jnp.zeros((32, ROWS), f32)
    for tile in range(tiles):
        span = slice(tile * TA, tile * TA + TA)
        copies[tile].wait()
        scores = jnp.where(mask[span, :] > 0, dot(q_own[span], all_keys), MASKED)
        weight = jnp.exp2(scores)
        local_p = weight.astype(bf16)
        local_g = (weight * dot(g_own[span], all_values)).astype(bf16)
        result[0:32, span] = (SCALE * (grad_query[:, span] + dot_nt(key_t, local_g))).astype(bf16)
        result[32:64, span] = (attended[:, span] + dot_nt(value_t, local_p)).astype(bf16)
        grad_k = grad_k + dot(q_t[:, span], local_g)
        grad_v = grad_v + dot(g_t[:, span], local_p)
    local[0:32, :] = SCALE * grad_k
    local[32:64, :] = grad_v
    copies[tiles].wait()
    out_term[...] = GRAD_SCALE * dot(result[32:64, :], cotangent[...])


def gather_kernel(arrived, places, local, result, rows_out, stacked_out, virt_out, near):
    found = split_places((places[0:1, :], places[1:2, :]))
    forward = scatter_rows(found, turn_parts(arrived[:, 0:32, :].reshape(ROWS, 128)))
    side = forward + spread_rows(arrived, 32, near).T
    keys_grad = (local[0:32, :] + side[0:32] + side[32:64]).astype(bf16)
    values_grad = (local[32:64, :] + side[64:96] + side[96:128]).astype(bf16)
    stacked = jnp.concatenate([result[0:32, :], keys_grad, values_grad, result[32:64, :]], axis=0)
    stacked_out[...] = stacked
    rows_out[:, 0:128, :] = stacked.astype(f32).T.astype(bf16).reshape(HEADS, 128, 128)
    parts = jnp.sum(arrived[:, 64:80, :].astype(f32), axis=0)
    virt = (parts + pltpu.roll(parts, 64, 1)).astype(bf16).astype(f32)
    inner = (lane((16, 128)) >= 32) & (lane((16, 128)) < 96)
    virt = jnp.where(inner, pltpu.roll(virt, 32, 1), 0.0)
    virt_out[...] = virt
    rows_out[:, 128:144, :] = jnp.broadcast_to(virt.astype(bf16)[None], (HEADS, 16, 128))


def partial_kernel(core, stacked, virt, feats, state, out_term, keep, give, held):
    virt = jnp.concatenate([virt[...], jnp.zeros((112, 128), f32)], axis=0)
    grads = dot(stacked[...], feats[...]) + dot(virt.T.astype(bf16), state[...])
    held[0] = GRAD_SCALE * grads[0:64]
    held[1, 0:32, :] = GRAD_SCALE * grads[64:96]
    held[1, 32:64, :] = out_term[...]
    keep[...] = held[core[0]]
    give[...] = held[1 - core[0]]


def mix_kernel(
    head, group, rows, weights0, weights2, weights6, weights1, weights7, feats_at, cotangent_at,
    columns, virt_out, feats, cotangent, turned, sems,
):
    which = head[0]
    span = pl.ds(pl.multiple_of(which * 128, 128), 128)
    copies = [
        pltpu.make_async_copy(feats_at.at[span], feats, sems.at[0]),
        pltpu.make_async_copy(cotangent_at.at[span], cotangent, sems.at[1]),
    ]
    for copy in copies:
        copy.start()
    grads = jnp.zeros((144, WIDTH), f32)
    mixed = jnp.zeros((128, WIDTH), f32)
    inner = lane((144, 128)) < 96
    sources = {0: weights0, 4: weights0, 1: weights1, 5: weights1, 7: weights7, 3: weights7}
    sources.update({2: weights2, 6: weights6})
    for turn, source in sources.items():
        row = rows[(which + turn) & 7]
        zero = jnp.zeros_like(row)
        at = 128 if turn in (3, 4, 5) else 0
        weight = source[at : at + 128, :]
        grads = grads + dot(jnp.where(inner, row, zero), weight)
        mixed = mixed + dot(jnp.where(inner, zero, row)[0:128], weight)
    turned[...] = jnp.concatenate([grads[128:144], jnp.zeros((112, WIDTH), f32)], axis=0).T
    own = turned[pl.ds(pl.multiple_of(which * 32, 32), 32), :]
    virt_out[...] = pltpu.roll(own, 16 * group[0], 1)
    for copy in copies:
        copy.wait()
    grads = (cotangent[...].astype(f32) + grads[0:128]).T
    mixed = (feats[...].astype(f32) + mixed).T.astype(bf16)
    hi = grads.astype(bf16)
    low = (grads - hi.astype(f32)).astype(bf16)
    columns[:, 0:32, :] = mixed.reshape(HEADS, 32, 128)
    columns[:, 32:64, :] = hi.reshape(HEADS, 32, 128)
    columns[:, 64:96, :] = low.reshape(HEADS, 32, 128)


def finish_kernel(
    core, columns, near, far, virt0, virt1, virt2, virt3, member,
    mixed, grad_feats, grad_qkv, grad_out, grad_virtual, held,
):
    held[core[0]] = near[...]
    held[1 - core[0]] = far[...]
    grad_qkv[0:64, :] = held[0]
    grad_qkv[64:96, :] = held[1, 0:32, :]
    grad_out[...] = held[1, 32:64, :]
    virt = (virt0[...] + virt1[...]) + (virt2[...] + virt3[...])
    grad_virtual[...] = virt[:, :VIRT]
    lookup = POOL_SCALE * dot3(virt, hot(member[...] == iota((128, ROWS), 0)))
    for h in range(HEADS):
        at = slice(128 * h, 128 * h + 128)
        mixed[:, at] = columns[h, 0:32, :]
        whole = columns[h, 32:64, :].astype(f32) + columns[h, 64:96, :].astype(f32)
        grad_feats[:, at] = (whole + lookup[:, at]).astype(bf16)


def array(shape, kind):
    return jax.ShapeDtypeStruct(shape, kind)


VMEM = pl.BlockSpec(memory_space=pltpu.VMEM)
SMEM = pl.BlockSpec(memory_space=pltpu.SMEM)
HBM = pl.BlockSpec(memory_space=pltpu.HBM)


def call(kernel, specs, outs, scratch=(), mib=48, **named):
    return pl.pallas_call(
        kernel,
        out_shape=outs,
        in_specs=specs,
        out_specs=jax.tree.map(lambda _: VMEM, outs),
        scratch_shapes=list(scratch),
        compiler_params=pltpu.CompilerParams(vmem_limit_bytes=mib * 1024 * 1024),
        **named,
    )


def exchange(x, axis):
    return lax.all_to_all(x, axis, split_axis=0, concat_axis=0, tiled=True)


def swap(x, axis, k):
    return lax.ppermute(x, axis, [(i, i ^ k) for i in range(lax.axis_size(axis))])


def shift(x, k):
    return lax.ppermute(x, "head", [((h + k) % HEADS, h) for h in range(HEADS)])


def shards(feats, w_qkv, w_out, virt_embed, member, expander, local_mask, cotangent):
    slab = lax.axis_index("dom").astype(i32).reshape(1)
    head = lax.axis_index("head").astype(i32).reshape(1)
    members = member.reshape(1, ROWS)
    first = call(
        pool_kernel,
        [HBM] * 3,
        array((SLABS, 8, 128), f32),
        scratch=[
            pltpu.VMEM((ROWS, WIDTH), bf16),
            pltpu.VMEM((1, ROWS), i32),
            pltpu.VMEM((2, ROWS), i32),
            pltpu.SemaphoreType.DMA((3,)),
        ],
        mib=60,
    )(feats, members, expander.T)
    feats_late, first = lax.optimization_barrier([feats, first])
    first = exchange(first, "dom")
    table, kv_weights, share, embed, query_t, grad_t, table_t = call(
        project_kernel,
        [VMEM] * 5,
        (
            array((ROWS, 128), bf16),
            array((128, WIDTH), bf16),
            array((128, WIDTH), bf16),
            array((VIRT, WIDTH), bf16),
            array((32, ROWS), bf16),
            array((32, ROWS), bf16),
            array((64, ROWS), bf16),
        ),
    )(feats_late, cotangent, jnp.transpose(w_qkv, (0, 2, 1)), w_out, virt_embed)
    second, places, state = call(
        rows_kernel,
        [SMEM] + [VMEM] * 5,
        (array((SLABS, 80, 128), bf16), array((8, ROWS), f32), array((128, WIDTH), bf16)),
        scratch=[pltpu.VMEM((ROWS, 128), f32)],
    )(slab, first, table, table_t, embed, kv_weights)
    second, share, query_t = lax.optimization_barrier([second, share, query_t])
    two = jnp.concatenate([share, swap(share, "head", 4)], axis=0)
    across = lambda rows: pl.BlockSpec((rows, TI), lambda i: (0, i))
    stats = pl.pallas_call(
        local_kernel,
        grid=(ROWS // TI,),
        out_shape=array((8, ROWS), f32),
        in_specs=[across(32), across(32), pl.BlockSpec((TI, ROWS), lambda i: (i, 0)), VMEM],
        out_specs=across(8),
        compiler_params=pltpu.CompilerParams(vmem_limit_bytes=52 * 1024 * 1024),
    )(query_t, grad_t, local_mask, table_t)
    second, two, stats = lax.optimization_barrier([exchange(second, "dom"), two, stats])
    third, parts, attended, grad_query = call(
        side_kernel,
        [VMEM] * 5,
        (
            array((SLABS, 80, 128), bf16),
            array((8, ROWS), f32),
            array((32, ROWS), f32),
            array((32, ROWS), f32),
        ),
        scratch=[pltpu.VMEM((ROWS, 128), f32)],
    )(query_t, grad_t, stats, second, places)
    local, result, out_term = call(
        attend_kernel,
        [VMEM] * 6 + [HBM] * 2,
        (array((64, ROWS), f32), array((64, ROWS), bf16), array((32, WIDTH), f32)),
        scratch=[
            pltpu.VMEM((ROWS, WIDTH), bf16),
            pltpu.VMEM((ROWS, ROWS), i32),
            pltpu.SemaphoreType.DMA((ROWS // TA + 1,)),
        ],
        mib=52,
    )(parts, attended, grad_query, query_t, grad_t, table_t, cotangent, local_mask)
    third, two, share = lax.optimization_barrier([third, two, share])
    others = [shift(share, 2), shift(share, 6), shift(two, 1), shift(two, 7)]
    third = exchange(third, "dom")
    rows, stacked, virt = call(
        gather_kernel,
        [VMEM] * 4,
        (array((HEADS, 144, 128), bf16), array((128, ROWS), bf16), array((16, 128), f32)),
        scratch=[
            pltpu.VMEM((ROWS, 128), f32),
        ],
    )(third, places, local, result)
    rows, stacked, *others = lax.optimization_barrier([rows, stacked] + others)
    rows = exchange(rows, "head")
    keep, give = call(
        partial_kernel,
        [SMEM] + [VMEM] * 5,
        (array((64, WIDTH), f32), array((64, WIDTH), f32)),
        scratch=[pltpu.VMEM((2, 64, WIDTH), f32)],
    )(slab & 1, stacked, virt, feats, state, out_term)
    keep = keep + swap(give, "dom", 1)
    keep = (keep + swap(keep, "dom", 2)) + (swap(keep, "dom", 4) + swap(keep, "dom", 6))
    rows, keep = lax.optimization_barrier([rows, keep])
    columns, virt = call(
        mix_kernel,
        [SMEM] * 2 + [VMEM] * 6 + [HBM] * 2,
        (array((HEADS, 96, 128), bf16), array((32, 128), f32)),
        scratch=[
            pltpu.VMEM((128, WIDTH), bf16),
            pltpu.VMEM((128, WIDTH), bf16),
            pltpu.VMEM((WIDTH, 128), f32),
            pltpu.SemaphoreType.DMA((2,)),
        ],
    )(head, slab & 3, rows, two, *others, feats, cotangent)
    columns = exchange(columns, "head")
    keep = (keep + swap(keep, "dom", 8)) + (swap(keep, "dom", 16) + swap(keep, "dom", 24))
    virts = [virt] + [swap(virt, "dom", k) for k in (1, 2, 3)]
    mixed, grad_feats, grad_qkv, grad_out, grad_virtual = call(
        finish_kernel,
        [SMEM] + [VMEM] * 8,
        (
            array((32, ROWS), bf16),
            array((32, ROWS), bf16),
            array((96, WIDTH), f32),
            array((32, WIDTH), f32),
            array((32, VIRT), f32),
        ),
        scratch=[pltpu.VMEM((2, 64, WIDTH), f32)],
    )(slab & 1, columns, keep, swap(keep, "dom", 1), *virts, members)
    grad_qkv = jnp.transpose(grad_qkv.reshape(3, 32, WIDTH), (0, 2, 1))
    return (mixed.T, grad_feats.T, grad_qkv, grad_out, grad_virtual.T)


def solution(mesh):
    return jax.shard_map(
        shards,
        mesh=mesh,
        in_specs=(
            P("dom", None),
            P(None, None, "head"),
            P("head", None),
            P(),
            P("dom"),
            P("dom", None),
            P("dom", None),
            P("dom", None),
        ),
        out_specs=(
            P("dom", "head"),
            P("dom", "head"),
            P(None, None, "head"),
            P("head", None),
            P(None, "head"),
        ),
        check_vma=False,
    )
```

```python
import functools

import jax
import jax.numpy as jnp
from jax import lax
from jax.experimental import pallas as pl
from jax.experimental.pallas import tpu as pltpu
from jax.sharding import PartitionSpec as P

HD = 32
VIRT = 64
SLABS = 32
HEADS = 8
ROWS = 1024
WIDTH = 256
NODES = SLABS * ROWS
BLOCK = ROWS // SLABS
SCALE = HD ** (-0.5)
POOL_SCALE = (VIRT / NODES) ** 0.5
GRAD_SCALE = NODES ** (-0.5)
TI = 256
TA = 256
MASKED = -1e30
LOG2E = 1.4426950408889634
SCALE2 = SCALE * LOG2E

f32 = jnp.float32
bf16 = jnp.bfloat16
i32 = jnp.int32


def dot(a, b):
    return jnp.dot(a, b, preferred_element_type=f32)


def dot_nt(a, b):
    return lax.dot_general(a, b, (((1,), (1,)), ((), ())), preferred_element_type=f32)


def iota(shape, dim):
    return lax.broadcasted_iota(i32, shape, dim)


def hot(cond):
    return jnp.where(cond, 1.0, 0.0).astype(bf16)


def split3(x):
    hi = x.astype(bf16)
    rest = x - hi.astype(f32)
    mid = rest.astype(bf16)
    low = (rest - mid.astype(f32)).astype(bf16)
    return hi, mid, low


def dot3(x, one_hot):
    rows = x.shape[0]
    got = dot(jnp.concatenate(split3(x), axis=0), one_hot)
    return got[:rows] + got[rows : 2 * rows] + got[2 * rows :]


def lane(shape):
    return iota(shape, len(shape) - 1)


def first_virt(slab):
    return 16 * (slab & 3) + 2 * (slab >> 2)


def branch0(shape):
    return (lane(shape) & 32) == 0


def place_rows(table):
    whole = table.astype(i32)
    hi = (whole >> 5).astype(f32).astype(bf16)
    low = (whole & 31).astype(f32).astype(bf16)
    shape = (SLABS, ROWS)
    own = (iota(shape, 1) >> 5) == iota(shape, 0)
    rows = []
    for e in range(2):
        pick = hot(iota((128, ROWS), 0) == 32 * e + (iota((128, ROWS), 1) & 31))
        full = dot(jnp.concatenate([hi, low], axis=0), pick)
        full = 32.0 * full[:SLABS] + full[SLABS:]
        rows.append(jnp.sum(jnp.where(own, full, 0.0), axis=0, keepdims=True))
    return rows


def pool_kernel(feats_at, member_at, expander_at, out, feats, member, expander, sems):
    copies = [
        pltpu.make_async_copy(source, target, sems.at[k])
        for k, (source, target) in enumerate(
            ((feats_at, feats), (member_at, member), (expander_at, expander))
        )
    ]
    for copy in copies:
        copy.start()
    copies[2].wait()
    out[...] = jnp.zeros(out.shape, f32)
    shape = (SLABS, ROWS)
    total = jnp.zeros((SLABS, 128), f32)
    for e in range(2):
        target = expander[e : e + 1, :]
        own = (iota(shape, 1) & 31) == ((iota(shape, 0) - e) & 31)
        hi = jnp.where(own, ((target >> 5) & 31).astype(f32), 0.0).astype(bf16)
        low = jnp.where(own, (target & 31).astype(f32), 0.0).astype(bf16)
        slot = hot((iota((ROWS, 128), 0) >> 5) + 32 * e == iota((ROWS, 128), 1))
        total = total + 32.0 * dot(hi, slot) + dot(low, slot)
    out[:, 4, :] = total
    copies[1].wait()
    shape = (VIRT, ROWS)
    order = iota(shape, 0)
    own = hot(member[...] == first_virt(order & 31) + (order >> 5))
    copies[0].wait()
    pooled = dot(own, feats[...])
    out[:, 0, :] = pooled[:32, :128]
    out[:, 1, :] = pooled[:32, 128:]
    out[:, 2, :] = pooled[32:, :128]
    out[:, 3, :] = pooled[32:, 128:]


def project_kernel(
    feats, cotangent, w_qkv, w_out, embed_in,
    table, kv_weights, share, embed, query_t, grad_t, table_t,
):
    embed[...] = embed_in[...]
    w_q, w_k, w_v = w_qkv[0], w_qkv[1], w_qkv[2]
    w_kv4 = jnp.concatenate([w_k, w_k, w_v, w_v], axis=0)
    kv_weights[...] = w_kv4
    share[...] = jnp.concatenate([w_q, w_k, w_v, w_out[...]], axis=0)
    table[...] = dot_nt(feats[...], w_kv4).astype(bf16)
    query_t[...] = dot_nt(w_q, feats[...]).astype(bf16)
    grad_t[...] = dot_nt(w_out[...], cotangent[...]).astype(bf16)
    table_t[...] = dot_nt(jnp.concatenate([w_k, w_v], axis=0), feats[...]).astype(bf16)


def turn_parts(x):
    turned = x.astype(f32).T
    return (
        jnp.concatenate([turned[0:32], turned[64:96]], axis=0),
        jnp.concatenate([turned[32:64], turned[96:128]], axis=0),
    )


def join_parts(parts):
    first, second = parts
    return jnp.concatenate([first[0:32], second[0:32], first[32:64], second[32:64]], axis=0)


def split_places(places):
    at = iota((256, 128), 0)
    found = []
    for place in places:
        whole = place.astype(i32)
        low = whole & 255
        cols = [hot(at == low[:, 128 * c : 128 * c + 128]) for c in range(8)]
        found.append((whole >> 8, jnp.concatenate(cols, axis=1)))
    return found


def gather_rows(found, pair):
    parts = []
    for (high, low_hot), part in zip(found, pair):
        part = part.astype(bf16)
        left = jnp.concatenate([part[:, 256 * k : 256 * k + 256] for k in range(4)], axis=0)
        got = dot(left, low_hot)
        chosen = got[192:256]
        for k in range(3):
            chosen = jnp.where(high == k, got[64 * k : 64 * k + 64], chosen)
        parts.append(chosen)
    return join_parts(parts)


def scatter_rows(found, pair):
    parts = []
    for (high, low_hot), part in zip(found, pair):
        left = jnp.concatenate([jnp.where(high == k, part, 0.0) for k in range(4)], axis=0)
        got = dot_nt(left.astype(bf16), low_hot)
        parts.append(jnp.concatenate([got[64 * k : 64 * k + 64] for k in range(4)], axis=1))
    return join_parts(parts)


def to_slabs(turned):
    return turned.T.astype(bf16).reshape(SLABS, BLOCK, 128)


def rows_kernel(slab, arrived, table, table_t, virt_embed, kv_weights, out, places, state, wide):
    row0, row1 = place_rows(arrived[:, 4, :])
    at = iota((8, ROWS), 0)
    places[...] = jnp.where(at == 0, row0, jnp.where(at == 1, row1, 0.0))
    shape = (8, VIRT)
    pick = hot((iota(shape, 1) == first_virt(slab[0]) + iota(shape, 0)) & (iota(shape, 0) < 2))
    embed = dot(pick, virt_embed[...])
    pooled = jnp.sum(arrived[...], axis=0)
    first = jnp.concatenate([pooled[0:1], pooled[1:2]], axis=1)
    second = jnp.concatenate([pooled[2:3], pooled[3:4]], axis=1)
    at = iota((8, WIDTH), 0)
    pooled = jnp.where(at == 0, first, jnp.where(at == 1, second, 0.0))
    virt_state = embed + POOL_SCALE * pooled
    at = iota((128, WIDTH), 0) - 2 * (slab[0] >> 2)
    whole = jnp.where(at == 0, virt_state[0:1], jnp.where(at == 1, virt_state[1:2], 0.0))
    state[...] = whole.astype(bf16)
    virt_state = jnp.concatenate([virt_state, jnp.zeros((8, WIDTH), f32)], axis=0).astype(bf16)
    virt_rows = dot_nt(virt_state, kv_weights[...]).astype(bf16)
    out[:, 64:80, :] = jnp.broadcast_to(virt_rows[None], (SLABS, 16, 128))
    wide[...] = table[...].astype(f32)
    leave_rows(wide, out)
    out[:, 32:64, :] = to_slabs(gather_rows(split_places((row0, row1)), (table_t[...],) * 2))


def spread_rows(arrived, at, held):
    blocks = [arrived[s, at : at + 32, :].astype(f32) for s in range(SLABS)]
    low_branch = branch0((BLOCK, 128))
    for s in range(SLABS):
        block = jnp.where(low_branch, blocks[s], blocks[(s + 1) % SLABS])
        held[pl.ds(s, BLOCK, stride=SLABS), :] = block
    return held[...]


def leave_rows(held, out):
    low_branch = branch0((BLOCK, 128))
    blocks = [held[pl.ds(s, BLOCK, stride=SLABS), :] for s in range(SLABS)]
    for s in range(SLABS):
        block = jnp.where(low_branch, blocks[s], blocks[(s - 1) % SLABS])
        out[s, 0:32, :] = block.astype(bf16)


def right_tables(table_t):
    key, value = table_t[0:32, :], table_t[32:64, :]
    at = iota((16, ROWS), 0)
    none = jnp.zeros((16, ROWS), bf16)
    less_base = jnp.where(at < 3, -1.0, 0.0).astype(bf16)
    less_centre = jnp.where((at >= 3) & (at < 6), -1.0, 0.0).astype(bf16)
    keys = jnp.concatenate([key, key, key, less_base, none], axis=0)
    values = jnp.concatenate([none, none, none, none, value, less_centre, none], axis=0)
    return keys, values


def left_query(query, parts):
    wide = [part.astype(f32) for part in split3(query.astype(f32) * SCALE2)]
    rest = jnp.zeros((24, query.shape[1]), f32)
    return jnp.concatenate(wide + [parts, rest], axis=0).T.astype(bf16)


def left_grad(grad, parts):
    rest = jnp.zeros((24, grad.shape[1]), f32)
    front = jnp.zeros((64, grad.shape[1]), f32)
    return jnp.concatenate([front, grad.astype(f32), parts, rest], axis=0).T.astype(bf16)


def stack_rows(rows, fill):
    at = iota((8, ROWS), 0)
    block = jnp.full((8, ROWS), fill, f32)
    for k, row in enumerate(rows):
        block = jnp.where(at == k, row, block)
    return block


def local_kernel(query_t, grad_t, mask, table_t, stats):
    none = jnp.zeros((8, TI), f32)
    q_own = left_query(query_t[...], none)
    g_own = left_grad(grad_t[...], none)
    keys, values = right_tables(table_t)
    scores = jnp.where(mask[...] > 0, dot(q_own, keys), MASKED)
    highest = jnp.max(scores, axis=1, keepdims=True)
    weight = jnp.exp2(scores - highest)
    value_dots = dot(g_own, values)
    total = jnp.sum(weight, axis=1, keepdims=True)
    centre = jnp.sum(weight * value_dots, axis=1, keepdims=True)
    at = lane((TI, 128))
    stat = jnp.where(at == 0, highest, jnp.where(at == 1, total, centre))
    stats[...] = stat.T[0:8]


def side_kernel(
    query_t, grad_t, stats, arrived, places,
    out, parts_out, attended_out, grad_query_out,
    near,
):
    virt_rows = arrived[:, 64:80, :].astype(f32)
    pieces = [virt_rows[4 * ((v & 15) >> 1) + (v >> 4), 0:2, :] for v in range(0, VIRT, 2)]
    virt_rows = jnp.concatenate(pieces, axis=0)
    at = lane((VIRT, 128))
    virt_left = jnp.where(at < 64, virt_rows, 0.0), jnp.where(at >= 64, virt_rows, 0.0)
    virt_left = jnp.concatenate(virt_left, axis=0).astype(bf16)
    virt_t = jnp.concatenate([virt_rows, jnp.zeros((64, 128), f32)], axis=0).T.astype(bf16)
    found = split_places((places[0:1, :], places[1:2, :]))
    forward = spread_rows(arrived, 32, near).T
    inverse = scatter_rows(found, turn_parts(arrived[:, 0:32, :].reshape(ROWS, 128)))
    side_k = (forward[0:32], forward[32:64], inverse[0:32], inverse[32:64])
    side_v = (forward[64:96], forward[96:128], inverse[64:96], inverse[96:128])
    q_t, g_t = query_t[...], grad_t[...]
    q_wide, g_wide = q_t.astype(f32), g_t.astype(f32)
    none = jnp.zeros((32, ROWS), bf16)
    virt = dot(virt_left, jnp.concatenate([q_t, none, g_t, none], axis=0))
    virt_s, virt_d = SCALE2 * virt[0:VIRT], virt[VIRT:]
    side_s = [SCALE2 * jnp.sum(q_wide * part, axis=0, keepdims=True) for part in side_k]
    side_d = [jnp.sum(g_wide * part, axis=0, keepdims=True) for part in side_v]
    side_s, side_d = stack_rows(side_s, MASKED), stack_rows(side_d, 0.0)
    local_m, local_t, local_c = stats[0:1, :], stats[1:2, :], stats[2:3, :]
    highest = jnp.maximum(jnp.max(virt_s, axis=0, keepdims=True), jnp.max(side_s, axis=0, keepdims=True))
    highest = jnp.maximum(local_m, highest)
    virt_p = jnp.exp2(virt_s - highest)
    side_p = jnp.exp2(side_s - highest)
    factor = jnp.exp2(local_m - highest)
    total = factor * local_t
    total = total + jnp.sum(virt_p, axis=0, keepdims=True) + jnp.sum(side_p, axis=0, keepdims=True)
    share = 1.0 / total
    virt_p = virt_p * share
    side_p = side_p * share
    centre = factor * share * local_c + jnp.sum(virt_p * virt_d, axis=0, keepdims=True)
    centre = centre + jnp.sum(side_p * side_d, axis=0, keepdims=True)
    base = highest + LOG2E * jnp.log(total)
    parts = [part.astype(f32) for column in (base, centre) for part in split3(column)]
    parts_out[...] = stack_rows(parts, 0.0)
    virt_g = (virt_p * (virt_d - centre)).astype(bf16)
    virt_p = virt_p.astype(bf16)
    side_g = (side_p * (side_d - centre)).astype(bf16).astype(f32)
    side_p = side_p.astype(bf16).astype(f32)
    attended = dot(virt_t[64:96, 0:VIRT], virt_p)
    grad_query = dot(virt_t[0:32, 0:VIRT], virt_g)
    key_terms, value_terms = [], []
    for k in range(4):
        one_p, one_g = side_p[k : k + 1], side_g[k : k + 1]
        attended = attended + one_p * side_v[k]
        grad_query = grad_query + one_g * side_k[k]
        key_terms.append((SCALE * (one_g * q_wide)).astype(bf16).astype(f32))
        value_terms.append((one_p * g_wide).astype(bf16).astype(f32))
    near[...] = jnp.concatenate(key_terms[:2] + value_terms[:2], axis=0).T
    leave_rows(near, out)
    pair = [jnp.concatenate([key_terms[k], value_terms[k]], axis=0) for k in (2, 3)]
    out[:, 32:64, :] = to_slabs(gather_rows(found, pair))
    sums = jnp.concatenate([SCALE * dot_nt(q_t, virt_g), dot_nt(g_t, virt_p)], axis=0)
    hi = sums.astype(bf16).astype(f32)
    both_parts = jnp.concatenate([hi, sums - hi], axis=0)
    both_parts = jnp.concatenate([both_parts, jnp.zeros((128, 64), f32)], axis=1).T[0:VIRT]
    both_parts = both_parts.astype(bf16)
    for slab in range(SLABS):
        first = 16 * (slab & 3)
        out[slab, 64:80, :] = both_parts[first : first + 16]
    attended_out[...] = attended
    grad_query_out[...] = grad_query


def attend_kernel(
    parts, attended, grad_query, query_t, grad_t, table_t, cotangent_at, mask_at,
    local, result, out_term,
    cotangent, mask, sems,
):
    tiles = ROWS // TA
    copies = []
    for tile in range(tiles):
        span = pl.ds(tile * TA, TA)
        copies.append(pltpu.make_async_copy(mask_at.at[span], mask.at[span], sems.at[tile]))
    copies.append(pltpu.make_async_copy(cotangent_at, cotangent, sems.at[tiles]))
    for copy in copies:
        copy.start()
    all_keys, all_values = right_tables(table_t)
    q_t, g_t = query_t[...], grad_t[...]
    q_own = left_query(q_t, parts[...])
    g_own = left_grad(g_t, parts[...])
    key_t, value_t = table_t[0:32, :], table_t[32:64, :]
    grad_k = jnp.zeros((32, ROWS), f32)
    grad_v = jnp.zeros((32, ROWS), f32)
    for tile in range(tiles):
        span = slice(tile * TA, tile * TA + TA)
        copies[tile].wait()
        scores = jnp.where(mask[span, :] > 0, dot(q_own[span], all_keys), MASKED)
        weight = jnp.exp2(scores)
        local_p = weight.astype(bf16)
        local_g = (weight * dot(g_own[span], all_values)).astype(bf16)
        result[0:32, span] = (SCALE * (grad_query[:, span] + dot_nt(key_t, local_g))).astype(bf16)
        result[32:64, span] = (attended[:, span] + dot_nt(value_t, local_p)).astype(bf16)
        grad_k = grad_k + dot(q_t[:, span], local_g)
        grad_v = grad_v + dot(g_t[:, span], local_p)
    local[0:32, :] = SCALE * grad_k
    local[32:64, :] = grad_v
    copies[tiles].wait()
    out_term[...] = GRAD_SCALE * dot(result[32:64, :], cotangent[...])


def gather_kernel(arrived, places, local, result, rows_out, stacked_out, virt_out, near):
    found = split_places((places[0:1, :], places[1:2, :]))
    forward = scatter_rows(found, turn_parts(arrived[:, 0:32, :].reshape(ROWS, 128)))
    side = forward + spread_rows(arrived, 32, near).T
    keys_grad = (local[0:32, :] + side[0:32] + side[32:64]).astype(bf16)
    values_grad = (local[32:64, :] + side[64:96] + side[96:128]).astype(bf16)
    stacked = jnp.concatenate([result[0:32, :], keys_grad, values_grad, result[32:64, :]], axis=0)
    stacked_out[...] = stacked
    rows_out[:, 0:128, :] = stacked.astype(f32).T.astype(bf16).reshape(HEADS, 128, 128)
    parts = jnp.sum(arrived[:, 64:80, :].astype(f32), axis=0)
    virt = (parts + pltpu.roll(parts, 64, 1)).astype(bf16).astype(f32)
    inner = (lane((16, 128)) >= 32) & (lane((16, 128)) < 96)
    virt = jnp.where(inner, pltpu.roll(virt, 32, 1), 0.0)
    virt_out[...] = virt
    rows_out[:, 128:144, :] = jnp.broadcast_to(virt.astype(bf16)[None], (HEADS, 16, 128))


def partial_kernel(core, stacked, virt, feats, state, out_term, keep, give, held):
    virt = jnp.concatenate([virt[...], jnp.zeros((112, 128), f32)], axis=0)
    grads = dot(stacked[...], feats[...]) + dot(virt.T.astype(bf16), state[...])
    held[0] = GRAD_SCALE * grads[0:64]
    held[1, 0:32, :] = GRAD_SCALE * grads[64:96]
    held[1, 32:64, :] = out_term[...]
    keep[...] = held[core[0]]
    give[...] = held[1 - core[0]]


def mix_kernel(
    head, group, rows, weights0, weights2, weights6, weights1, weights7, feats_at, cotangent_at,
    columns, virt_out, feats, cotangent, turned, sems,
):
    which = head[0]
    span = pl.ds(pl.multiple_of(which * 128, 128), 128)
    copies = [
        pltpu.make_async_copy(feats_at.at[span], feats, sems.at[0]),
        pltpu.make_async_copy(cotangent_at.at[span], cotangent, sems.at[1]),
    ]
    for copy in copies:
        copy.start()
    grads = jnp.zeros((144, WIDTH), f32)
    mixed = jnp.zeros((128, WIDTH), f32)
    inner = lane((144, 128)) < 96
    sources = {0: weights0, 4: weights0, 1: weights1, 5: weights1, 7: weights7, 3: weights7}
    sources.update({2: weights2, 6: weights6})
    turns = list(sources)
    for two in (turns[0:2], turns[2:4], turns[4:6], turns[6:8]):
        found = [rows[(which + turn) & 7] for turn in two]
        zero = jnp.zeros_like(found[0])
        weight = [sources[turn][pl.ds(128 if turn in (3, 4, 5) else 0, 128), :] for turn in two]
        weight = jnp.concatenate(weight, axis=0)
        left = jnp.concatenate([jnp.where(inner, row, zero) for row in found], axis=1)
        grads = grads + dot(left, weight)
        left = jnp.concatenate([jnp.where(inner, zero, row)[0:128] for row in found], axis=1)
        mixed = mixed + dot(left, weight)
    turned[...] = jnp.concatenate([grads[128:144], jnp.zeros((112, WIDTH), f32)], axis=0).T
    own = turned[pl.ds(pl.multiple_of(which * 32, 32), 32), :]
    virt_out[...] = pltpu.roll(own, 16 * group[0], 1)
    for copy in copies:
        copy.wait()
    grads = (cotangent[...].astype(f32) + grads[0:128]).T
    mixed = (feats[...].astype(f32) + mixed).T.astype(bf16)
    hi = grads.astype(bf16)
    low = (grads - hi.astype(f32)).astype(bf16)
    columns[:, 0:32, :] = mixed.reshape(HEADS, 32, 128)
    columns[:, 32:64, :] = hi.reshape(HEADS, 32, 128)
    columns[:, 64:96, :] = low.reshape(HEADS, 32, 128)


def finish_kernel(
    core, columns, near, far, virt0, virt1, virt2, virt3, member,
    mixed, grad_feats, grad_qkv, grad_out, grad_virtual, held,
):
    held[core[0]] = near[...]
    held[1 - core[0]] = far[...]
    grad_qkv[0:64, :] = held[0]
    grad_qkv[64:96, :] = held[1, 0:32, :]
    grad_out[...] = held[1, 32:64, :]
    virt = (virt0[...] + virt1[...]) + (virt2[...] + virt3[...])
    grad_virtual[...] = virt[:, :VIRT]
    lookup = POOL_SCALE * dot3(virt, hot(member[...] == iota((128, ROWS), 0)))
    for h in range(HEADS):
        at = slice(128 * h, 128 * h + 128)
        mixed[:, at] = columns[h, 0:32, :]
        whole = columns[h, 32:64, :].astype(f32) + columns[h, 64:96, :].astype(f32)
        grad_feats[:, at] = (whole + lookup[:, at]).astype(bf16)


def array(shape, kind):
    return jax.ShapeDtypeStruct(shape, kind)


VMEM = pl.BlockSpec(memory_space=pltpu.VMEM)
SMEM = pl.BlockSpec(memory_space=pltpu.SMEM)
HBM = pl.BlockSpec(memory_space=pltpu.HBM)


def call(kernel, specs, outs, scratch=(), mib=48, **named):
    return pl.pallas_call(
        kernel,
        out_shape=outs,
        in_specs=specs,
        out_specs=jax.tree.map(lambda _: VMEM, outs),
        scratch_shapes=list(scratch),
        compiler_params=pltpu.CompilerParams(vmem_limit_bytes=mib * 1024 * 1024),
        **named,
    )


def exchange(x, axis):
    return lax.all_to_all(x, axis, split_axis=0, concat_axis=0, tiled=True)


def swap(x, axis, k):
    return lax.ppermute(x, axis, [(i, i ^ k) for i in range(lax.axis_size(axis))])


def shift(x, k):
    return lax.ppermute(x, "head", [((h + k) % HEADS, h) for h in range(HEADS)])


def shards(feats, w_qkv, w_out, virt_embed, member, expander, local_mask, cotangent):
    slab = lax.axis_index("dom").astype(i32).reshape(1)
    head = lax.axis_index("head").astype(i32).reshape(1)
    members = member.reshape(1, ROWS)
    first = call(
        pool_kernel,
        [HBM] * 3,
        array((SLABS, 8, 128), f32),
        scratch=[
            pltpu.VMEM((ROWS, WIDTH), bf16),
            pltpu.VMEM((1, ROWS), i32),
            pltpu.VMEM((2, ROWS), i32),
            pltpu.SemaphoreType.DMA((3,)),
        ],
        mib=60,
    )(feats, members, expander.T)
    feats_late, first = lax.optimization_barrier([feats, first])
    first = exchange(first, "dom")
    table, kv_weights, share, embed, query_t, grad_t, table_t = call(
        project_kernel,
        [VMEM] * 5,
        (
            array((ROWS, 128), bf16),
            array((128, WIDTH), bf16),
            array((128, WIDTH), bf16),
            array((VIRT, WIDTH), bf16),
            array((32, ROWS), bf16),
            array((32, ROWS), bf16),
            array((64, ROWS), bf16),
        ),
    )(feats_late, cotangent, jnp.transpose(w_qkv, (0, 2, 1)), w_out, virt_embed)
    second, places, state = call(
        rows_kernel,
        [SMEM] + [VMEM] * 5,
        (array((SLABS, 80, 128), bf16), array((8, ROWS), f32), array((128, WIDTH), bf16)),
        scratch=[pltpu.VMEM((ROWS, 128), f32)],
    )(slab, first, table, table_t, embed, kv_weights)
    second, share, query_t = lax.optimization_barrier([second, share, query_t])
    two = jnp.concatenate([share, swap(share, "head", 4)], axis=0)
    across = lambda rows: pl.BlockSpec((rows, TI), lambda i: (0, i))
    stats = pl.pallas_call(
        local_kernel,
        grid=(ROWS // TI,),
        out_shape=array((8, ROWS), f32),
        in_specs=[across(32), across(32), pl.BlockSpec((TI, ROWS), lambda i: (i, 0)), VMEM],
        out_specs=across(8),
        compiler_params=pltpu.CompilerParams(vmem_limit_bytes=52 * 1024 * 1024),
    )(query_t, grad_t, local_mask, table_t)
    second, two, stats = lax.optimization_barrier([exchange(second, "dom"), two, stats])
    third, parts, attended, grad_query = call(
        side_kernel,
        [VMEM] * 5,
        (
            array((SLABS, 80, 128), bf16),
            array((8, ROWS), f32),
            array((32, ROWS), f32),
            array((32, ROWS), f32),
        ),
        scratch=[pltpu.VMEM((ROWS, 128), f32)],
    )(query_t, grad_t, stats, second, places)
    local, result, out_term = call(
        attend_kernel,
        [VMEM] * 6 + [HBM] * 2,
        (array((64, ROWS), f32), array((64, ROWS), bf16), array((32, WIDTH), f32)),
        scratch=[
            pltpu.VMEM((ROWS, WIDTH), bf16),
            pltpu.VMEM((ROWS, ROWS), i32),
            pltpu.SemaphoreType.DMA((ROWS // TA + 1,)),
        ],
        mib=52,
    )(parts, attended, grad_query, query_t, grad_t, table_t, cotangent, local_mask)
    third, two, share = lax.optimization_barrier([third, two, share])
    others = [shift(share, 2), shift(share, 6), shift(two, 1), shift(two, 7)]
    third = exchange(third, "dom")
    rows, stacked, virt = call(
        gather_kernel,
        [VMEM] * 4,
        (array((HEADS, 144, 128), bf16), array((128, ROWS), bf16), array((16, 128), f32)),
        scratch=[
            pltpu.VMEM((ROWS, 128), f32),
        ],
    )(third, places, local, result)
    rows, stacked, *others = lax.optimization_barrier([rows, stacked] + others)
    rows = exchange(rows, "head")
    keep, give = call(
        partial_kernel,
        [SMEM] + [VMEM] * 5,
        (array((64, WIDTH), f32), array((64, WIDTH), f32)),
        scratch=[pltpu.VMEM((2, 64, WIDTH), f32)],
    )(slab & 1, stacked, virt, feats, state, out_term)
    keep = keep + swap(give, "dom", 1)
    keep = (keep + swap(keep, "dom", 2)) + (swap(keep, "dom", 4) + swap(keep, "dom", 6))
    rows, keep = lax.optimization_barrier([rows, keep])
    columns, virt = call(
        mix_kernel,
        [SMEM] * 2 + [VMEM] * 6 + [HBM] * 2,
        (array((HEADS, 96, 128), bf16), array((32, 128), f32)),
        scratch=[
            pltpu.VMEM((128, WIDTH), bf16),
            pltpu.VMEM((128, WIDTH), bf16),
            pltpu.VMEM((WIDTH, 128), f32),
            pltpu.SemaphoreType.DMA((2,)),
        ],
    )(head, slab & 3, rows, two, *others, feats, cotangent)
    columns, keep = lax.optimization_barrier([columns, keep])
    columns = exchange(columns, "head")
    keep = (keep + swap(keep, "dom", 8)) + (swap(keep, "dom", 16) + swap(keep, "dom", 24))
    virts = [virt] + [swap(virt, "dom", k) for k in (1, 2, 3)]
    mixed, grad_feats, grad_qkv, grad_out, grad_virtual = call(
        finish_kernel,
        [SMEM] + [VMEM] * 8,
        (
            array((32, ROWS), bf16),
            array((32, ROWS), bf16),
            array((96, WIDTH), f32),
            array((32, WIDTH), f32),
            array((32, VIRT), f32),
        ),
        scratch=[pltpu.VMEM((2, 64, WIDTH), f32)],
    )(slab & 1, columns, keep, swap(keep, "dom", 1), *virts, members)
    grad_qkv = jnp.transpose(grad_qkv.reshape(3, 32, WIDTH), (0, 2, 1))
    return (mixed.T, grad_feats.T, grad_qkv, grad_out, grad_virtual.T)


def solution(mesh):
    return jax.shard_map(
        shards,
        mesh=mesh,
        in_specs=(
            P("dom", None),
            P(None, None, "head"),
            P("head", None),
            P(),
            P("dom"),
            P("dom", None),
            P("dom", None),
            P("dom", None),
        ),
        out_specs=(
            P("dom", "head"),
            P("dom", "head"),
            P(None, None, "head"),
            P("head", None),
            P(None, "head"),
        ),
        check_vma=False,
    )
```

```python
import functools

import jax
import jax.numpy as jnp
from jax import lax
from jax.experimental import pallas as pl
from jax.experimental.pallas import tpu as pltpu
from jax.sharding import PartitionSpec as P

HD = 32
VIRT = 64
SLABS = 32
HEADS = 8
ROWS = 1024
WIDTH = 256
NODES = SLABS * ROWS
BLOCK = ROWS // SLABS
SCALE = HD ** (-0.5)
POOL_SCALE = (VIRT / NODES) ** 0.5
GRAD_SCALE = NODES ** (-0.5)
TI = 256
TA = 256
MASKED = -1e30
LOG2E = 1.4426950408889634
SCALE2 = SCALE * LOG2E

f32 = jnp.float32
bf16 = jnp.bfloat16
i32 = jnp.int32


def dot(a, b):
    return jnp.dot(a, b, preferred_element_type=f32)


def dot_nt(a, b):
    return lax.dot_general(a, b, (((1,), (1,)), ((), ())), preferred_element_type=f32)


def iota(shape, dim):
    return lax.broadcasted_iota(i32, shape, dim)


def hot(cond):
    return jnp.where(cond, 1.0, 0.0).astype(bf16)


def split3(x):
    hi = x.astype(bf16)
    rest = x - hi.astype(f32)
    mid = rest.astype(bf16)
    low = (rest - mid.astype(f32)).astype(bf16)
    return hi, mid, low


def dot3(x, one_hot):
    rows = x.shape[0]
    got = dot(jnp.concatenate(split3(x), axis=0), one_hot)
    return got[:rows] + got[rows : 2 * rows] + got[2 * rows :]


def lane(shape):
    return iota(shape, len(shape) - 1)


def first_virt(slab):
    return 16 * (slab & 3) + 2 * (slab >> 2)


def branch0(shape):
    return (lane(shape) & 32) == 0


def place_rows(table):
    whole = table.astype(i32)
    hi = (whole >> 5).astype(f32).astype(bf16)
    low = (whole & 31).astype(f32).astype(bf16)
    shape = (SLABS, ROWS)
    own = (iota(shape, 1) >> 5) == iota(shape, 0)
    rows = []
    for e in range(2):
        pick = hot(iota((128, ROWS), 0) == 32 * e + (iota((128, ROWS), 1) & 31))
        full = dot(jnp.concatenate([hi, low], axis=0), pick)
        full = 32.0 * full[:SLABS] + full[SLABS:]
        rows.append(jnp.sum(jnp.where(own, full, 0.0), axis=0, keepdims=True))
    return rows


def pool_kernel(feats_at, member_at, expander_at, out, feats, member, expander, sems):
    copies = [
        pltpu.make_async_copy(source, target, sems.at[k])
        for k, (source, target) in enumerate(
            ((feats_at, feats), (member_at, member), (expander_at, expander))
        )
    ]
    for copy in copies:
        copy.start()
    copies[2].wait()
    out[...] = jnp.zeros(out.shape, f32)
    shape = (SLABS, ROWS)
    total = jnp.zeros((SLABS, 128), f32)
    for e in range(2):
        target = expander[e : e + 1, :]
        own = (iota(shape, 1) & 31) == ((iota(shape, 0) - e) & 31)
        hi = jnp.where(own, ((target >> 5) & 31).astype(f32), 0.0).astype(bf16)
        low = jnp.where(own, (target & 31).astype(f32), 0.0).astype(bf16)
        slot = hot((iota((ROWS, 128), 0) >> 5) + 32 * e == iota((ROWS, 128), 1))
        total = total + 32.0 * dot(hi, slot) + dot(low, slot)
    out[:, 4, :] = total
    copies[1].wait()
    shape = (VIRT, ROWS)
    order = iota(shape, 0)
    own = hot(member[...] == first_virt(order & 31) + (order >> 5))
    copies[0].wait()
    pooled = dot(own, feats[...])
    out[:, 0, :] = pooled[:32, :128]
    out[:, 1, :] = pooled[:32, 128:]
    out[:, 2, :] = pooled[32:, :128]
    out[:, 3, :] = pooled[32:, 128:]


def project_kernel(
    feats, cotangent, w_qkv, w_out, embed_in,
    table, kv_weights, share, embed, query_t, grad_t, table_t,
):
    embed[...] = embed_in[...]
    w_q, w_k, w_v = w_qkv[0], w_qkv[1], w_qkv[2]
    w_kv4 = jnp.concatenate([w_k, w_k, w_v, w_v], axis=0)
    kv_weights[...] = w_kv4
    share[...] = jnp.concatenate([w_q, w_k, w_v, w_out[...]], axis=0)
    table[...] = dot_nt(feats[...], w_kv4).astype(bf16)
    query_t[...] = dot_nt(w_q, feats[...]).astype(bf16)
    grad_t[...] = dot_nt(w_out[...], cotangent[...]).astype(bf16)
    table_t[...] = dot_nt(jnp.concatenate([w_k, w_v], axis=0), feats[...]).astype(bf16)


def turn_parts(x):
    turned = x.astype(f32).T
    return (
        jnp.concatenate([turned[0:32], turned[64:96]], axis=0),
        jnp.concatenate([turned[32:64], turned[96:128]], axis=0),
    )


def join_parts(parts):
    first, second = parts
    return jnp.concatenate([first[0:32], second[0:32], first[32:64], second[32:64]], axis=0)


def split_places(places):
    at = iota((256, 128), 0)
    found = []
    for place in places:
        whole = place.astype(i32)
        low = whole & 255
        cols = [hot(at == low[:, 128 * c : 128 * c + 128]) for c in range(8)]
        found.append((whole >> 8, jnp.concatenate(cols, axis=1)))
    return found


def gather_rows(found, pair):
    parts = []
    for (high, low_hot), part in zip(found, pair):
        part = part.astype(bf16)
        left = jnp.concatenate([part[:, 256 * k : 256 * k + 256] for k in range(4)], axis=0)
        got = dot(left, low_hot)
        chosen = got[192:256]
        for k in range(3):
            chosen = jnp.where(high == k, got[64 * k : 64 * k + 64], chosen)
        parts.append(chosen)
    return join_parts(parts)


def scatter_rows(found, pair):
    parts = []
    for (high, low_hot), part in zip(found, pair):
        left = jnp.concatenate([jnp.where(high == k, part, 0.0) for k in range(4)], axis=0)
        got = dot_nt(left.astype(bf16), low_hot)
        parts.append(jnp.concatenate([got[64 * k : 64 * k + 64] for k in range(4)], axis=1))
    return join_parts(parts)


def to_slabs(turned):
    return turned.T.astype(bf16).reshape(SLABS, BLOCK, 128)


def rows_kernel(slab, arrived, table, table_t, virt_embed, kv_weights, out, places, state, wide):
    row0, row1 = place_rows(arrived[:, 4, :])
    at = iota((8, ROWS), 0)
    places[...] = jnp.where(at == 0, row0, jnp.where(at == 1, row1, 0.0))
    shape = (8, VIRT)
    pick = hot((iota(shape, 1) == first_virt(slab[0]) + iota(shape, 0)) & (iota(shape, 0) < 2))
    embed = dot(pick, virt_embed[...])
    pooled = jnp.sum(arrived[...], axis=0)
    first = jnp.concatenate([pooled[0:1], pooled[1:2]], axis=1)
    second = jnp.concatenate([pooled[2:3], pooled[3:4]], axis=1)
    at = iota((8, WIDTH), 0)
    pooled = jnp.where(at == 0, first, jnp.where(at == 1, second, 0.0))
    virt_state = embed + POOL_SCALE * pooled
    at = iota((128, WIDTH), 0) - 2 * (slab[0] >> 2)
    whole = jnp.where(at == 0, virt_state[0:1], jnp.where(at == 1, virt_state[1:2], 0.0))
    state[...] = whole.astype(bf16)
    virt_state = jnp.concatenate([virt_state, jnp.zeros((8, WIDTH), f32)], axis=0).astype(bf16)
    virt_rows = dot_nt(virt_state, kv_weights[...]).astype(bf16)
    out[:, 64:80, :] = jnp.broadcast_to(virt_rows[None], (SLABS, 16, 128))
    wide[...] = table[...].astype(f32)
    leave_rows(wide, out)
    out[:, 32:64, :] = to_slabs(gather_rows(split_places((row0, row1)), (table_t[...],) * 2))


def spread_rows(arrived, at, held):
    blocks = [arrived[s, at : at + 32, :].astype(f32) for s in range(SLABS)]
    low_branch = branch0((BLOCK, 128))
    for s in range(SLABS):
        block = jnp.where(low_branch, blocks[s], blocks[(s + 1) % SLABS])
        held[pl.ds(s, BLOCK, stride=SLABS), :] = block
    return held[...]


def leave_rows(held, out):
    low_branch = branch0((BLOCK, 128))
    blocks = [held[pl.ds(s, BLOCK, stride=SLABS), :] for s in range(SLABS)]
    for s in range(SLABS):
        block = jnp.where(low_branch, blocks[s], blocks[(s - 1) % SLABS])
        out[s, 0:32, :] = block.astype(bf16)


def right_tables(table_t):
    key, value = table_t[0:32, :], table_t[32:64, :]
    at = iota((16, ROWS), 0)
    none = jnp.zeros((16, ROWS), bf16)
    less_base = jnp.where(at < 3, -1.0, 0.0).astype(bf16)
    less_centre = jnp.where((at >= 3) & (at < 6), -1.0, 0.0).astype(bf16)
    keys = jnp.concatenate([key, key, key, less_base, none], axis=0)
    values = jnp.concatenate([none, none, none, none, value, less_centre, none], axis=0)
    return keys, values


def left_query(query, parts):
    wide = [part.astype(f32) for part in split3(query.astype(f32) * SCALE2)]
    rest = jnp.zeros((24, query.shape[1]), f32)
    return jnp.concatenate(wide + [parts, rest], axis=0).T.astype(bf16)


def left_grad(grad, parts):
    rest = jnp.zeros((24, grad.shape[1]), f32)
    front = jnp.zeros((64, grad.shape[1]), f32)
    return jnp.concatenate([front, grad.astype(f32), parts, rest], axis=0).T.astype(bf16)


def stack_rows(rows, fill):
    at = iota((8, ROWS), 0)
    block = jnp.full((8, ROWS), fill, f32)
    for k, row in enumerate(rows):
        block = jnp.where(at == k, row, block)
    return block


def local_kernel(query_t, grad_t, mask, table_t, stats):
    none = jnp.zeros((8, TI), f32)
    q_own = left_query(query_t[...], none)
    g_own = left_grad(grad_t[...], none)
    keys, values = right_tables(table_t)
    scores = jnp.where(mask[...] > 0, dot(q_own, keys), MASKED)
    highest = jnp.max(scores, axis=1, keepdims=True)
    weight = jnp.exp2(scores - highest)
    value_dots = dot(g_own, values)
    total = jnp.sum(weight, axis=1, keepdims=True)
    centre = jnp.sum(weight * value_dots, axis=1, keepdims=True)
    at = lane((TI, 128))
    stat = jnp.where(at == 0, highest, jnp.where(at == 1, total, centre))
    stats[...] = stat.T[0:8]


def side_kernel(
    query_t, grad_t, stats, arrived, places,
    out, parts_out, attended_out, grad_query_out,
    near,
):
    virt_rows = arrived[:, 64:80, :].astype(f32)
    pieces = [virt_rows[4 * ((v & 15) >> 1) + (v >> 4), 0:2, :] for v in range(0, VIRT, 2)]
    virt_rows = jnp.concatenate(pieces, axis=0)
    at = lane((VIRT, 128))
    virt_left = jnp.where(at < 64, virt_rows, 0.0), jnp.where(at >= 64, virt_rows, 0.0)
    virt_left = jnp.concatenate(virt_left, axis=0).astype(bf16)
    virt_t = jnp.concatenate([virt_rows, jnp.zeros((64, 128), f32)], axis=0).T.astype(bf16)
    found = split_places((places[0:1, :], places[1:2, :]))
    forward = spread_rows(arrived, 32, near).T
    inverse = scatter_rows(found, turn_parts(arrived[:, 0:32, :].reshape(ROWS, 128)))
    side_k = (forward[0:32], forward[32:64], inverse[0:32], inverse[32:64])
    side_v = (forward[64:96], forward[96:128], inverse[64:96], inverse[96:128])
    q_t, g_t = query_t[...], grad_t[...]
    q_wide, g_wide = q_t.astype(f32), g_t.astype(f32)
    none = jnp.zeros((32, ROWS), bf16)
    virt = dot(virt_left, jnp.concatenate([q_t, none, g_t, none], axis=0))
    virt_s, virt_d = SCALE2 * virt[0:VIRT], virt[VIRT:]
    side_s = [SCALE2 * jnp.sum(q_wide * part, axis=0, keepdims=True) for part in side_k]
    side_d = [jnp.sum(g_wide * part, axis=0, keepdims=True) for part in side_v]
    side_s, side_d = stack_rows(side_s, MASKED), stack_rows(side_d, 0.0)
    local_m, local_t, local_c = stats[0:1, :], stats[1:2, :], stats[2:3, :]
    highest = jnp.maximum(jnp.max(virt_s, axis=0, keepdims=True), jnp.max(side_s, axis=0, keepdims=True))
    highest = jnp.maximum(local_m, highest)
    virt_p = jnp.exp2(virt_s - highest)
    side_p = jnp.exp2(side_s - highest)
    factor = jnp.exp2(local_m - highest)
    total = factor * local_t
    total = total + jnp.sum(virt_p, axis=0, keepdims=True) + jnp.sum(side_p, axis=0, keepdims=True)
    share = 1.0 / total
    virt_p = virt_p * share
    side_p = side_p * share
    centre = factor * share * local_c + jnp.sum(virt_p * virt_d, axis=0, keepdims=True)
    centre = centre + jnp.sum(side_p * side_d, axis=0, keepdims=True)
    base = highest + LOG2E * jnp.log(total)
    parts = [part.astype(f32) for column in (base, centre) for part in split3(column)]
    parts_out[...] = stack_rows(parts, 0.0)
    virt_g = (virt_p * (virt_d - centre)).astype(bf16)
    virt_p = virt_p.astype(bf16)
    side_g = (side_p * (side_d - centre)).astype(bf16).astype(f32)
    side_p = side_p.astype(bf16).astype(f32)
    attended = dot(virt_t[64:96, 0:VIRT], virt_p)
    grad_query = dot(virt_t[0:32, 0:VIRT], virt_g)
    key_terms, value_terms = [], []
    for k in range(4):
        one_p, one_g = side_p[k : k + 1], side_g[k : k + 1]
        attended = attended + one_p * side_v[k]
        grad_query = grad_query + one_g * side_k[k]
        key_terms.append((SCALE * (one_g * q_wide)).astype(bf16).astype(f32))
        value_terms.append((one_p * g_wide).astype(bf16).astype(f32))
    near[...] = jnp.concatenate(key_terms[:2] + value_terms[:2], axis=0).T
    leave_rows(near, out)
    pair = [jnp.concatenate([key_terms[k], value_terms[k]], axis=0) for k in (2, 3)]
    out[:, 32:64, :] = to_slabs(gather_rows(found, pair))
    sums = jnp.concatenate([SCALE * dot_nt(q_t, virt_g), dot_nt(g_t, virt_p)], axis=0)
    hi = sums.astype(bf16).astype(f32)
    both_parts = jnp.concatenate([hi, sums - hi], axis=0)
    both_parts = jnp.concatenate([both_parts, jnp.zeros((128, 64), f32)], axis=1).T[0:VIRT]
    both_parts = both_parts.astype(bf16)
    for slab in range(SLABS):
        first = 16 * (slab & 3)
        out[slab, 64:80, :] = both_parts[first : first + 16]
    attended_out[...] = attended
    grad_query_out[...] = grad_query


def attend_kernel(
    parts, attended, grad_query, query_t, grad_t, table_t, cotangent_at, mask_at,
    local, result, out_term,
    cotangent, mask, sems,
):
    tiles = ROWS // TA
    copies = []
    for tile in range(tiles):
        span = pl.ds(tile * TA, TA)
        copies.append(pltpu.make_async_copy(mask_at.at[span], mask.at[span], sems.at[tile]))
    copies.append(pltpu.make_async_copy(cotangent_at, cotangent, sems.at[tiles]))
    for copy in copies:
        copy.start()
    all_keys, all_values = right_tables(table_t)
    q_t, g_t = query_t[...], grad_t[...]
    q_own = left_query(q_t, parts[...])
    g_own = left_grad(g_t, parts[...])
    key_t, value_t = table_t[0:32, :], table_t[32:64, :]
    grad_k = jnp.zeros((32, ROWS), f32)
    grad_v = jnp.zeros((32, ROWS), f32)
    for tile in range(tiles):
        span = slice(tile * TA, tile * TA + TA)
        copies[tile].wait()
        scores = jnp.where(mask[span, :] > 0, dot(q_own[span], all_keys), MASKED)
        weight = jnp.exp2(scores)
        local_p = weight.astype(bf16)
        local_g = (weight * dot(g_own[span], all_values)).astype(bf16)
        result[0:32, span] = (SCALE * (grad_query[:, span] + dot_nt(key_t, local_g))).astype(bf16)
        result[32:64, span] = (attended[:, span] + dot_nt(value_t, local_p)).astype(bf16)
        grad_k = grad_k + dot(q_t[:, span], local_g)
        grad_v = grad_v + dot(g_t[:, span], local_p)
    local[0:32, :] = SCALE * grad_k
    local[32:64, :] = grad_v
    copies[tiles].wait()
    out_term[...] = GRAD_SCALE * dot(result[32:64, :], cotangent[...])


def gather_kernel(arrived, places, local, result, rows_out, stacked_out, virt_out, near):
    found = split_places((places[0:1, :], places[1:2, :]))
    forward = scatter_rows(found, turn_parts(arrived[:, 0:32, :].reshape(ROWS, 128)))
    side = forward + spread_rows(arrived, 32, near).T
    keys_grad = (local[0:32, :] + side[0:32] + side[32:64]).astype(bf16)
    values_grad = (local[32:64, :] + side[64:96] + side[96:128]).astype(bf16)
    stacked = jnp.concatenate([result[0:32, :], keys_grad, values_grad, result[32:64, :]], axis=0)
    stacked_out[...] = stacked
    rows_out[:, 0:128, :] = stacked.astype(f32).T.astype(bf16).reshape(HEADS, 128, 128)
    parts = jnp.sum(arrived[:, 64:80, :].astype(f32), axis=0)
    virt = (parts + pltpu.roll(parts, 64, 1)).astype(bf16).astype(f32)
    inner = (lane((16, 128)) >= 32) & (lane((16, 128)) < 96)
    virt = jnp.where(inner, pltpu.roll(virt, 32, 1), 0.0)
    virt_out[...] = virt
    rows_out[:, 128:144, :] = jnp.broadcast_to(virt.astype(bf16)[None], (HEADS, 16, 128))


def partial_kernel(core, stacked, virt, feats, state, out_term, keep, give, held):
    virt = jnp.concatenate([virt[...], jnp.zeros((112, 128), f32)], axis=0)
    grads = dot(stacked[...], feats[...]) + dot(virt.T.astype(bf16), state[...])
    held[0] = GRAD_SCALE * grads[0:64]
    held[1, 0:32, :] = GRAD_SCALE * grads[64:96]
    held[1, 32:64, :] = out_term[...]
    keep[...] = held[core[0]]
    give[...] = held[1 - core[0]]


def mix_kernel(
    head, group, rows, weights0, weights2, weights6, weights1, weights7, feats_at, cotangent_at,
    columns, virt_out, feats, cotangent, turned, sems,
):
    which = head[0]
    span = pl.ds(pl.multiple_of(which * 128, 128), 128)
    copies = [
        pltpu.make_async_copy(feats_at.at[span], feats, sems.at[0]),
        pltpu.make_async_copy(cotangent_at.at[span], cotangent, sems.at[1]),
    ]
    for copy in copies:
        copy.start()
    grads = jnp.zeros((144, WIDTH), f32)
    mixed = jnp.zeros((128, WIDTH), f32)
    inner = lane((144, 128)) < 96
    sources = {0: weights0, 4: weights0, 1: weights1, 5: weights1, 7: weights7, 3: weights7}
    sources.update({2: weights2, 6: weights6})
    turns = list(sources)
    for two in (turns[0:2], turns[2:4], turns[4:6], turns[6:8]):
        found = [rows[(which + turn) & 7] for turn in two]
        zero = jnp.zeros_like(found[0])
        weight = [sources[turn][pl.ds(128 if turn in (3, 4, 5) else 0, 128), :] for turn in two]
        weight = jnp.concatenate(weight, axis=0)
        left = jnp.concatenate([jnp.where(inner, row, zero) for row in found], axis=1)
        grads = grads + dot(left, weight)
        left = jnp.concatenate([jnp.where(inner, zero, row)[0:128] for row in found], axis=1)
        mixed = mixed + dot(left, weight)
    turned[...] = jnp.concatenate([grads[128:144], jnp.zeros((112, WIDTH), f32)], axis=0).T
    own = turned[pl.ds(pl.multiple_of(which * 32, 32), 32), :]
    virt_out[...] = pltpu.roll(own, 16 * group[0], 1)
    for copy in copies:
        copy.wait()
    grads = (cotangent[...].astype(f32) + grads[0:128]).T
    mixed = (feats[...].astype(f32) + mixed).T.astype(bf16)
    hi = grads.astype(bf16)
    low = (grads - hi.astype(f32)).astype(bf16)
    columns[:, 0:32, :] = mixed.reshape(HEADS, 32, 128)
    columns[:, 32:64, :] = hi.reshape(HEADS, 32, 128)
    columns[:, 64:96, :] = low.reshape(HEADS, 32, 128)


def finish_kernel(
    core, columns, near, far, virt0, virt1, virt2, virt3, member,
    mixed, grad_feats, grad_qkv, grad_out, grad_virtual, held,
):
    held[core[0]] = near[...]
    held[1 - core[0]] = far[...]
    grad_qkv[0:64, :] = held[0]
    grad_qkv[64:96, :] = held[1, 0:32, :]
    grad_out[...] = held[1, 32:64, :]
    virt = (virt0[...] + virt1[...]) + (virt2[...] + virt3[...])
    grad_virtual[...] = virt[:, :VIRT]
    lookup = POOL_SCALE * dot3(virt, hot(member[...] == iota((128, ROWS), 0)))
    for h in range(HEADS):
        at = slice(128 * h, 128 * h + 128)
        mixed[:, at] = columns[h, 0:32, :]
        whole = columns[h, 32:64, :].astype(f32) + columns[h, 64:96, :].astype(f32)
        grad_feats[:, at] = (whole + lookup[:, at]).astype(bf16)


def array(shape, kind):
    return jax.ShapeDtypeStruct(shape, kind)


VMEM = pl.BlockSpec(memory_space=pltpu.VMEM)
SMEM = pl.BlockSpec(memory_space=pltpu.SMEM)
HBM = pl.BlockSpec(memory_space=pltpu.HBM)


def call(kernel, specs, outs, scratch=(), mib=48, **named):
    return pl.pallas_call(
        kernel,
        out_shape=outs,
        in_specs=specs,
        out_specs=jax.tree.map(lambda _: VMEM, outs),
        scratch_shapes=list(scratch),
        compiler_params=pltpu.CompilerParams(vmem_limit_bytes=mib * 1024 * 1024),
        **named,
    )


def exchange(x, axis):
    return lax.all_to_all(x, axis, split_axis=0, concat_axis=0, tiled=True)


def swap(x, axis, k):
    return lax.ppermute(x, axis, [(i, i ^ k) for i in range(lax.axis_size(axis))])


def shift(x, k):
    return lax.ppermute(x, "head", [((h + k) % HEADS, h) for h in range(HEADS)])


def shards(feats, w_qkv, w_out, virt_embed, member, expander, local_mask, cotangent):
    slab = lax.axis_index("dom").astype(i32).reshape(1)
    head = lax.axis_index("head").astype(i32).reshape(1)
    members = member.reshape(1, ROWS)
    first = call(
        pool_kernel,
        [HBM] * 3,
        array((SLABS, 8, 128), f32),
        scratch=[
            pltpu.VMEM((ROWS, WIDTH), bf16),
            pltpu.VMEM((1, ROWS), i32),
            pltpu.VMEM((2, ROWS), i32),
            pltpu.SemaphoreType.DMA((3,)),
        ],
        mib=60,
    )(feats, members, expander.T)
    feats_late, first = lax.optimization_barrier([feats, first])
    first = exchange(first, "dom")
    table, kv_weights, share, embed, query_t, grad_t, table_t = call(
        project_kernel,
        [VMEM] * 5,
        (
            array((ROWS, 128), bf16),
            array((128, WIDTH), bf16),
            array((128, WIDTH), bf16),
            array((VIRT, WIDTH), bf16),
            array((32, ROWS), bf16),
            array((32, ROWS), bf16),
            array((64, ROWS), bf16),
        ),
    )(feats_late, cotangent, jnp.transpose(w_qkv, (0, 2, 1)), w_out, virt_embed)
    second, places, state = call(
        rows_kernel,
        [SMEM] + [VMEM] * 5,
        (array((SLABS, 80, 128), bf16), array((8, ROWS), f32), array((128, WIDTH), bf16)),
        scratch=[pltpu.VMEM((ROWS, 128), f32)],
    )(slab, first, table, table_t, embed, kv_weights)
    second, share, query_t = lax.optimization_barrier([second, share, query_t])
    two = jnp.concatenate([share, swap(share, "head", 4)], axis=0)
    across = lambda rows: pl.BlockSpec((rows, TI), lambda i: (0, i))
    stats = pl.pallas_call(
        local_kernel,
        grid=(ROWS // TI,),
        out_shape=array((8, ROWS), f32),
        in_specs=[across(32), across(32), pl.BlockSpec((TI, ROWS), lambda i: (i, 0)), VMEM],
        out_specs=across(8),
        compiler_params=pltpu.CompilerParams(vmem_limit_bytes=52 * 1024 * 1024),
    )(query_t, grad_t, local_mask, table_t)
    after = shift(share, 2)
    second, two, after, stats = lax.optimization_barrier([exchange(second, "dom"), two, after, stats])
    third, parts, attended, grad_query = call(
        side_kernel,
        [VMEM] * 5,
        (
            array((SLABS, 80, 128), bf16),
            array((8, ROWS), f32),
            array((32, ROWS), f32),
            array((32, ROWS), f32),
        ),
        scratch=[pltpu.VMEM((ROWS, 128), f32)],
    )(query_t, grad_t, stats, second, places)
    local, result, out_term = call(
        attend_kernel,
        [VMEM] * 6 + [HBM] * 2,
        (array((64, ROWS), f32), array((64, ROWS), bf16), array((32, WIDTH), f32)),
        scratch=[
            pltpu.VMEM((ROWS, WIDTH), bf16),
            pltpu.VMEM((ROWS, ROWS), i32),
            pltpu.SemaphoreType.DMA((ROWS // TA + 1,)),
        ],
        mib=52,
    )(parts, attended, grad_query, query_t, grad_t, table_t, cotangent, local_mask)
    third, two, share = lax.optimization_barrier([third, two, share])
    others = [shift(share, 6), shift(two, 1), shift(two, 7)]
    third = exchange(third, "dom")
    rows, stacked, virt = call(
        gather_kernel,
        [VMEM] * 4,
        (array((HEADS, 144, 128), bf16), array((128, ROWS), bf16), array((16, 128), f32)),
        scratch=[
            pltpu.VMEM((ROWS, 128), f32),
        ],
    )(third, places, local, result)
    rows, stacked, *others = lax.optimization_barrier([rows, stacked] + others)
    rows = exchange(rows, "head")
    keep, give = call(
        partial_kernel,
        [SMEM] + [VMEM] * 5,
        (array((64, WIDTH), f32), array((64, WIDTH), f32)),
        scratch=[pltpu.VMEM((2, 64, WIDTH), f32)],
    )(slab & 1, stacked, virt, feats, state, out_term)
    keep = keep + swap(give, "dom", 1)
    keep = (keep + swap(keep, "dom", 2)) + (swap(keep, "dom", 4) + swap(keep, "dom", 6))
    rows, keep = lax.optimization_barrier([rows, keep])
    columns, virt = call(
        mix_kernel,
        [SMEM] * 2 + [VMEM] * 6 + [HBM] * 2,
        (array((HEADS, 96, 128), bf16), array((32, 128), f32)),
        scratch=[
            pltpu.VMEM((128, WIDTH), bf16),
            pltpu.VMEM((128, WIDTH), bf16),
            pltpu.VMEM((WIDTH, 128), f32),
            pltpu.SemaphoreType.DMA((2,)),
        ],
    )(head, slab & 3, rows, two, after, *others, feats, cotangent)
    columns, keep = lax.optimization_barrier([columns, keep])
    columns = exchange(columns, "head")
    keep = (keep + swap(keep, "dom", 8)) + (swap(keep, "dom", 16) + swap(keep, "dom", 24))
    virts = [virt] + [swap(virt, "dom", k) for k in (1, 2, 3)]
    mixed, grad_feats, grad_qkv, grad_out, grad_virtual = call(
        finish_kernel,
        [SMEM] + [VMEM] * 8,
        (
            array((32, ROWS), bf16),
            array((32, ROWS), bf16),
            array((96, WIDTH), f32),
            array((32, WIDTH), f32),
            array((32, VIRT), f32),
        ),
        scratch=[pltpu.VMEM((2, 64, WIDTH), f32)],
    )(slab & 1, columns, keep, swap(keep, "dom", 1), *virts, members)
    grad_qkv = jnp.transpose(grad_qkv.reshape(3, 32, WIDTH), (0, 2, 1))
    return (mixed.T, grad_feats.T, grad_qkv, grad_out, grad_virtual.T)


def solution(mesh):
    return jax.shard_map(
        shards,
        mesh=mesh,
        in_specs=(
            P("dom", None),
            P(None, None, "head"),
            P("head", None),
            P(),
            P("dom"),
            P("dom", None),
            P("dom", None),
            P("dom", None),
        ),
        out_specs=(
            P("dom", "head"),
            P("dom", "head"),
            P(None, None, "head"),
            P("head", None),
            P(None, "head"),
        ),
        check_vma=False,
    )
```

```python
import functools

import jax
import jax.numpy as jnp
from jax import lax
from jax.experimental import pallas as pl
from jax.experimental.pallas import tpu as pltpu
from jax.sharding import PartitionSpec as P

HD = 32
VIRT = 64
SLABS = 32
HEADS = 8
ROWS = 1024
WIDTH = 256
NODES = SLABS * ROWS
BLOCK = ROWS // SLABS
SCALE = HD ** (-0.5)
POOL_SCALE = (VIRT / NODES) ** 0.5
GRAD_SCALE = NODES ** (-0.5)
TI = 256
TA = 256
MASKED = -1e30
LOG2E = 1.4426950408889634
SCALE2 = SCALE * LOG2E

f32 = jnp.float32
bf16 = jnp.bfloat16
i32 = jnp.int32


def dot(a, b):
    return jnp.dot(a, b, preferred_element_type=f32)


def dot_nt(a, b):
    return lax.dot_general(a, b, (((1,), (1,)), ((), ())), preferred_element_type=f32)


def iota(shape, dim):
    return lax.broadcasted_iota(i32, shape, dim)


def hot(cond):
    return jnp.where(cond, 1.0, 0.0).astype(bf16)


def split3(x):
    hi = x.astype(bf16)
    rest = x - hi.astype(f32)
    mid = rest.astype(bf16)
    low = (rest - mid.astype(f32)).astype(bf16)
    return hi, mid, low


def dot3(x, one_hot):
    rows = x.shape[0]
    got = dot(jnp.concatenate(split3(x), axis=0), one_hot)
    return got[:rows] + got[rows : 2 * rows] + got[2 * rows :]


def lane(shape):
    return iota(shape, len(shape) - 1)


def first_virt(slab):
    return 16 * (slab & 3) + 2 * (slab >> 2)


def branch0(shape):
    return (lane(shape) & 32) == 0


def place_rows(table):
    whole = table.astype(i32)
    hi = (whole >> 5).astype(f32).astype(bf16)
    low = (whole & 31).astype(f32).astype(bf16)
    shape = (SLABS, ROWS)
    own = (iota(shape, 1) >> 5) == iota(shape, 0)
    rows = []
    for e in range(2):
        pick = hot(iota((128, ROWS), 0) == 32 * e + (iota((128, ROWS), 1) & 31))
        full = dot(jnp.concatenate([hi, low], axis=0), pick)
        full = 32.0 * full[:SLABS] + full[SLABS:]
        rows.append(jnp.sum(jnp.where(own, full, 0.0), axis=0, keepdims=True))
    return rows


def pool_kernel(feats_at, member_at, expander_at, out, feats, member, expander, sems):
    copies = [
        pltpu.make_async_copy(source, target, sems.at[k])
        for k, (source, target) in enumerate(
            ((feats_at, feats), (member_at, member), (expander_at, expander))
        )
    ]
    for copy in copies:
        copy.start()
    copies[2].wait()
    out[...] = jnp.zeros(out.shape, f32)
    shape = (SLABS, ROWS)
    total = jnp.zeros((SLABS, 128), f32)
    for e in range(2):
        target = expander[e : e + 1, :]
        own = (iota(shape, 1) & 31) == ((iota(shape, 0) - e) & 31)
        hi = jnp.where(own, ((target >> 5) & 31).astype(f32), 0.0).astype(bf16)
        low = jnp.where(own, (target & 31).astype(f32), 0.0).astype(bf16)
        slot = hot((iota((ROWS, 128), 0) >> 5) + 32 * e == iota((ROWS, 128), 1))
        total = total + 32.0 * dot(hi, slot) + dot(low, slot)
    out[:, 4, :] = total
    copies[1].wait()
    shape = (VIRT, ROWS)
    order = iota(shape, 0)
    own = hot(member[...] == first_virt(order & 31) + (order >> 5))
    copies[0].wait()
    pooled = dot(own, feats[...])
    out[:, 0, :] = pooled[:32, :128]
    out[:, 1, :] = pooled[:32, 128:]
    out[:, 2, :] = pooled[32:, :128]
    out[:, 3, :] = pooled[32:, 128:]


def project_kernel(
    feats, cotangent, w_qkv, w_out, embed_in,
    table, kv_weights, share, embed, query_t, grad_t, table_t,
):
    embed[...] = embed_in[...]
    w_q, w_k, w_v = w_qkv[0], w_qkv[1], w_qkv[2]
    w_kv4 = jnp.concatenate([w_k, w_k, w_v, w_v], axis=0)
    kv_weights[...] = w_kv4
    share[...] = jnp.concatenate([w_q, w_k, w_v, w_out[...]], axis=0)
    table[...] = dot_nt(feats[...], w_kv4).astype(bf16)
    query_t[...] = dot_nt(w_q, feats[...]).astype(bf16)
    grad_t[...] = dot_nt(w_out[...], cotangent[...]).astype(bf16)
    table_t[...] = dot_nt(jnp.concatenate([w_k, w_v], axis=0), feats[...]).astype(bf16)


def turn_parts(x):
    turned = x.astype(f32).T
    return (
        jnp.concatenate([turned[0:32], turned[64:96]], axis=0),
        jnp.concatenate([turned[32:64], turned[96:128]], axis=0),
    )


def join_parts(parts):
    first, second = parts
    return jnp.concatenate([first[0:32], second[0:32], first[32:64], second[32:64]], axis=0)


def split_places(places):
    at = iota((256, 128), 0)
    found = []
    for place in places:
        whole = place.astype(i32)
        low = whole & 255
        cols = [hot(at == low[:, 128 * c : 128 * c + 128]) for c in range(8)]
        found.append((whole >> 8, jnp.concatenate(cols, axis=1)))
    return found


def gather_rows(found, pair):
    parts = []
    for (high, low_hot), part in zip(found, pair):
        part = part.astype(bf16)
        left = jnp.concatenate([part[:, 256 * k : 256 * k + 256] for k in range(4)], axis=0)
        got = dot(left, low_hot)
        chosen = got[192:256]
        for k in range(3):
            chosen = jnp.where(high == k, got[64 * k : 64 * k + 64], chosen)
        parts.append(chosen)
    return join_parts(parts)


def scatter_rows(found, pair):
    parts = []
    for (high, low_hot), part in zip(found, pair):
        left = jnp.concatenate([jnp.where(high == k, part, 0.0) for k in range(4)], axis=0)
        got = dot_nt(left.astype(bf16), low_hot)
        parts.append(jnp.concatenate([got[64 * k : 64 * k + 64] for k in range(4)], axis=1))
    return join_parts(parts)


def to_slabs(turned):
    return turned.T.astype(bf16).reshape(SLABS, BLOCK, 128)


def rows_kernel(slab, arrived, table, table_t, virt_embed, kv_weights, out, places, state, wide):
    row0, row1 = place_rows(arrived[:, 4, :])
    at = iota((8, ROWS), 0)
    places[...] = jnp.where(at == 0, row0, jnp.where(at == 1, row1, 0.0))
    shape = (8, VIRT)
    pick = hot((iota(shape, 1) == first_virt(slab[0]) + iota(shape, 0)) & (iota(shape, 0) < 2))
    embed = dot(pick, virt_embed[...])
    pooled = jnp.sum(arrived[...], axis=0)
    first = jnp.concatenate([pooled[0:1], pooled[1:2]], axis=1)
    second = jnp.concatenate([pooled[2:3], pooled[3:4]], axis=1)
    at = iota((8, WIDTH), 0)
    pooled = jnp.where(at == 0, first, jnp.where(at == 1, second, 0.0))
    virt_state = embed + POOL_SCALE * pooled
    at = iota((128, WIDTH), 0) - 2 * (slab[0] >> 2)
    whole = jnp.where(at == 0, virt_state[0:1], jnp.where(at == 1, virt_state[1:2], 0.0))
    state[...] = whole.astype(bf16)
    virt_state = jnp.concatenate([virt_state, jnp.zeros((8, WIDTH), f32)], axis=0).astype(bf16)
    virt_rows = dot_nt(virt_state, kv_weights[...]).astype(bf16)
    out[:, 64:80, :] = jnp.broadcast_to(virt_rows[None], (SLABS, 16, 128))
    wide[...] = table[...].astype(f32)
    leave_rows(wide, out)
    out[:, 32:64, :] = to_slabs(gather_rows(split_places((row0, row1)), (table_t[...],) * 2))


def spread_rows(arrived, at, held):
    blocks = [arrived[s, at : at + 32, :].astype(f32) for s in range(SLABS)]
    low_branch = branch0((BLOCK, 128))
    for s in range(SLABS):
        block = jnp.where(low_branch, blocks[s], blocks[(s + 1) % SLABS])
        held[pl.ds(s, BLOCK, stride=SLABS), :] = block
    return held[...]


def leave_rows(held, out):
    low_branch = branch0((BLOCK, 128))
    blocks = [held[pl.ds(s, BLOCK, stride=SLABS), :] for s in range(SLABS)]
    for s in range(SLABS):
        block = jnp.where(low_branch, blocks[s], blocks[(s - 1) % SLABS])
        out[s, 0:32, :] = block.astype(bf16)


def right_tables(table_t):
    key, value = table_t[0:32, :], table_t[32:64, :]
    at = iota((16, ROWS), 0)
    none = jnp.zeros((16, ROWS), bf16)
    less_base = jnp.where(at < 3, -1.0, 0.0).astype(bf16)
    less_centre = jnp.where((at >= 3) & (at < 6), -1.0, 0.0).astype(bf16)
    keys = jnp.concatenate([key, key, key, less_base, none], axis=0)
    values = jnp.concatenate([none, none, none, none, value, less_centre, none], axis=0)
    return keys, values


def left_query(query, parts):
    wide = [part.astype(f32) for part in split3(query.astype(f32) * SCALE2)]
    rest = jnp.zeros((24, query.shape[1]), f32)
    return jnp.concatenate(wide + [parts, rest], axis=0).T.astype(bf16)


def left_grad(grad, parts):
    rest = jnp.zeros((24, grad.shape[1]), f32)
    front = jnp.zeros((64, grad.shape[1]), f32)
    return jnp.concatenate([front, grad.astype(f32), parts, rest], axis=0).T.astype(bf16)


def stack_rows(rows, fill):
    at = iota((8, ROWS), 0)
    block = jnp.full((8, ROWS), fill, f32)
    for k, row in enumerate(rows):
        block = jnp.where(at == k, row, block)
    return block


def local_kernel(query_t, grad_t, mask, table_t, stats):
    none = jnp.zeros((8, TI), f32)
    q_own = left_query(query_t[...], none)
    g_own = left_grad(grad_t[...], none)
    keys, values = right_tables(table_t)
    scores = jnp.where(mask[...] > 0, dot(q_own, keys), MASKED)
    highest = jnp.max(scores, axis=1, keepdims=True)
    weight = jnp.exp2(scores - highest)
    value_dots = dot(g_own, values)
    total = jnp.sum(weight, axis=1, keepdims=True)
    centre = jnp.sum(weight * value_dots, axis=1, keepdims=True)
    at = lane((TI, 128))
    stat = jnp.where(at == 0, highest, jnp.where(at == 1, total, centre))
    stats[...] = stat.T[0:8]


def side_kernel(
    query_t, grad_t, stats, arrived, places,
    out, parts_out, attended_out, grad_query_out,
    near,
):
    virt_rows = arrived[:, 64:80, :].astype(f32)
    pieces = [virt_rows[4 * ((v & 15) >> 1) + (v >> 4), 0:2, :] for v in range(0, VIRT, 2)]
    virt_rows = jnp.concatenate(pieces, axis=0)
    at = lane((VIRT, 128))
    virt_left = jnp.where(at < 64, virt_rows, 0.0), jnp.where(at >= 64, virt_rows, 0.0)
    virt_left = jnp.concatenate(virt_left, axis=0).astype(bf16)
    virt_t = jnp.concatenate([virt_rows, jnp.zeros((64, 128), f32)], axis=0).T.astype(bf16)
    found = split_places((places[0:1, :], places[1:2, :]))
    forward = spread_rows(arrived, 32, near).T
    inverse = scatter_rows(found, turn_parts(arrived[:, 0:32, :].reshape(ROWS, 128)))
    side_k = (forward[0:32], forward[32:64], inverse[0:32], inverse[32:64])
    side_v = (forward[64:96], forward[96:128], inverse[64:96], inverse[96:128])
    q_t, g_t = query_t[...], grad_t[...]
    q_wide, g_wide = q_t.astype(f32), g_t.astype(f32)
    none = jnp.zeros((32, ROWS), bf16)
    virt = dot(virt_left, jnp.concatenate([q_t, none, g_t, none], axis=0))
    virt_s, virt_d = SCALE2 * virt[0:VIRT], virt[VIRT:]
    side_s = [SCALE2 * jnp.sum(q_wide * part, axis=0, keepdims=True) for part in side_k]
    side_d = [jnp.sum(g_wide * part, axis=0, keepdims=True) for part in side_v]
    side_s, side_d = stack_rows(side_s, MASKED), stack_rows(side_d, 0.0)
    local_m, local_t, local_c = stats[0:1, :], stats[1:2, :], stats[2:3, :]
    highest = jnp.maximum(jnp.max(virt_s, axis=0, keepdims=True), jnp.max(side_s, axis=0, keepdims=True))
    highest = jnp.maximum(local_m, highest)
    virt_p = jnp.exp2(virt_s - highest)
    side_p = jnp.exp2(side_s - highest)
    factor = jnp.exp2(local_m - highest)
    total = factor * local_t
    total = total + jnp.sum(virt_p, axis=0, keepdims=True) + jnp.sum(side_p, axis=0, keepdims=True)
    share = 1.0 / total
    virt_p = virt_p * share
    side_p = side_p * share
    centre = factor * share * local_c + jnp.sum(virt_p * virt_d, axis=0, keepdims=True)
    centre = centre + jnp.sum(side_p * side_d, axis=0, keepdims=True)
    base = highest + LOG2E * jnp.log(total)
    parts = [part.astype(f32) for column in (base, centre) for part in split3(column)]
    parts_out[...] = stack_rows(parts, 0.0)
    virt_g = (virt_p * (virt_d - centre)).astype(bf16)
    virt_p = virt_p.astype(bf16)
    side_g = (side_p * (side_d - centre)).astype(bf16).astype(f32)
    side_p = side_p.astype(bf16).astype(f32)
    attended = dot(virt_t[64:96, 0:VIRT], virt_p)
    grad_query = dot(virt_t[0:32, 0:VIRT], virt_g)
    key_terms, value_terms = [], []
    for k in range(4):
        one_p, one_g = side_p[k : k + 1], side_g[k : k + 1]
        attended = attended + one_p * side_v[k]
        grad_query = grad_query + one_g * side_k[k]
        key_terms.append((SCALE * (one_g * q_wide)).astype(bf16).astype(f32))
        value_terms.append((one_p * g_wide).astype(bf16).astype(f32))
    near[...] = jnp.concatenate(key_terms[:2] + value_terms[:2], axis=0).T
    leave_rows(near, out)
    pair = [jnp.concatenate([key_terms[k], value_terms[k]], axis=0) for k in (2, 3)]
    out[:, 32:64, :] = to_slabs(gather_rows(found, pair))
    sums = jnp.concatenate([SCALE * dot_nt(q_t, virt_g), dot_nt(g_t, virt_p)], axis=0)
    hi = sums.astype(bf16).astype(f32)
    both_parts = jnp.concatenate([hi, sums - hi], axis=0)
    both_parts = jnp.concatenate([both_parts, jnp.zeros((128, 64), f32)], axis=1).T[0:VIRT]
    both_parts = both_parts.astype(bf16)
    for slab in range(SLABS):
        first = 16 * (slab & 3)
        out[slab, 64:80, :] = both_parts[first : first + 16]
    attended_out[...] = attended
    grad_query_out[...] = grad_query


def attend_kernel(
    parts, attended, grad_query, query_t, grad_t, table_t, cotangent_at, mask_at,
    local, result, out_term,
    cotangent, mask, sems,
):
    tiles = ROWS // TA
    copies = []
    for tile in range(tiles):
        span = pl.ds(tile * TA, TA)
        copies.append(pltpu.make_async_copy(mask_at.at[span], mask.at[span], sems.at[tile]))
    copies.append(pltpu.make_async_copy(cotangent_at, cotangent, sems.at[tiles]))
    for copy in copies:
        copy.start()
    all_keys, all_values = right_tables(table_t)
    q_t, g_t = query_t[...], grad_t[...]
    q_own = left_query(q_t, parts[...])
    g_own = left_grad(g_t, parts[...])
    key_t, value_t = table_t[0:32, :], table_t[32:64, :]
    grad_k = jnp.zeros((32, ROWS), f32)
    grad_v = jnp.zeros((32, ROWS), f32)
    for tile in range(tiles):
        span = slice(tile * TA, tile * TA + TA)
        copies[tile].wait()
        scores = jnp.where(mask[span, :] > 0, dot(q_own[span], all_keys), MASKED)
        weight = jnp.exp2(scores)
        local_p = weight.astype(bf16)
        local_g = (weight * dot(g_own[span], all_values)).astype(bf16)
        result[0:32, span] = (SCALE * (grad_query[:, span] + dot_nt(key_t, local_g))).astype(bf16)
        result[32:64, span] = (attended[:, span] + dot_nt(value_t, local_p)).astype(bf16)
        grad_k = grad_k + dot(q_t[:, span], local_g)
        grad_v = grad_v + dot(g_t[:, span], local_p)
    local[0:32, :] = SCALE * grad_k
    local[32:64, :] = grad_v
    copies[tiles].wait()
    out_term[...] = GRAD_SCALE * dot(result[32:64, :], cotangent[...])


def gather_kernel(arrived, places, local, result, rows_out, stacked_out, virt_out, near):
    found = split_places((places[0:1, :], places[1:2, :]))
    forward = scatter_rows(found, turn_parts(arrived[:, 0:32, :].reshape(ROWS, 128)))
    side = forward + spread_rows(arrived, 32, near).T
    keys_grad = (local[0:32, :] + side[0:32] + side[32:64]).astype(bf16)
    values_grad = (local[32:64, :] + side[64:96] + side[96:128]).astype(bf16)
    stacked = jnp.concatenate([result[0:32, :], keys_grad, values_grad, result[32:64, :]], axis=0)
    stacked_out[...] = stacked
    rows_out[:, 0:128, :] = stacked.astype(f32).T.astype(bf16).reshape(HEADS, 128, 128)
    parts = jnp.sum(arrived[:, 64:80, :].astype(f32), axis=0)
    virt = (parts + pltpu.roll(parts, 64, 1)).astype(bf16).astype(f32)
    inner = (lane((16, 128)) >= 32) & (lane((16, 128)) < 96)
    virt = jnp.where(inner, pltpu.roll(virt, 32, 1), 0.0)
    virt_out[...] = virt
    rows_out[:, 128:144, :] = jnp.broadcast_to(virt.astype(bf16)[None], (HEADS, 16, 128))


def partial_kernel(core, stacked, virt, feats, state, out_term, keep, give, held):
    virt = jnp.concatenate([virt[...], jnp.zeros((112, 128), f32)], axis=0)
    grads = dot(stacked[...], feats[...]) + dot(virt.T.astype(bf16), state[...])
    held[0] = GRAD_SCALE * grads[0:64]
    held[1, 0:32, :] = GRAD_SCALE * grads[64:96]
    held[1, 32:64, :] = out_term[...]
    keep[...] = held[core[0]]
    give[...] = held[1 - core[0]]


def mix_kernel(
    head, group, rows, weights0, weights2, weights6, weights1, weights7, feats_at, cotangent_at,
    columns, virt_out, feats, cotangent, turned, sems,
):
    which = head[0]
    span = pl.ds(pl.multiple_of(which * 128, 128), 128)
    copies = [
        pltpu.make_async_copy(feats_at.at[span], feats, sems.at[0]),
        pltpu.make_async_copy(cotangent_at.at[span], cotangent, sems.at[1]),
    ]
    for copy in copies:
        copy.start()
    grads = jnp.zeros((144, WIDTH), f32)
    mixed = jnp.zeros((128, WIDTH), f32)
    inner = lane((144, 128)) < 96
    sources = {0: weights0, 4: weights0, 1: weights1, 5: weights1, 7: weights7, 3: weights7}
    sources.update({2: weights2, 6: weights6})
    turns = list(sources)
    for two in (turns[0:2], turns[2:4], turns[4:6], turns[6:8]):
        found = [rows[(which + turn) & 7] for turn in two]
        zero = jnp.zeros_like(found[0])
        weight = [sources[turn][pl.ds(128 if turn in (3, 4, 5) else 0, 128), :] for turn in two]
        weight = jnp.concatenate(weight, axis=0)
        left = jnp.concatenate([jnp.where(inner, row, zero) for row in found], axis=1)
        grads = grads + dot(left, weight)
        left = jnp.concatenate([jnp.where(inner, zero, row)[0:128] for row in found], axis=1)
        mixed = mixed + dot(left, weight)
    turned[...] = jnp.concatenate([grads[128:144], jnp.zeros((112, WIDTH), f32)], axis=0).T
    own = turned[pl.ds(pl.multiple_of(which * 32, 32), 32), :]
    virt_out[...] = pltpu.roll(own, 16 * group[0], 1)
    for copy in copies:
        copy.wait()
    grads = (cotangent[...].astype(f32) + grads[0:128]).T
    mixed = (feats[...].astype(f32) + mixed).T.astype(bf16)
    hi = grads.astype(bf16)
    low = (grads - hi.astype(f32)).astype(bf16)
    columns[:, 0:32, :] = mixed.reshape(HEADS, 32, 128)
    columns[:, 32:64, :] = hi.reshape(HEADS, 32, 128)
    columns[:, 64:96, :] = low.reshape(HEADS, 32, 128)


def finish_kernel(
    core, columns, both, virt0, virt1, virt2, virt3, member,
    mixed, grad_feats, grad_qkv, grad_out, grad_virtual, held,
):
    held[core[0]] = both[0:64, :]
    held[1 - core[0]] = both[64:128, :]
    grad_qkv[0:64, :] = held[0]
    grad_qkv[64:96, :] = held[1, 0:32, :]
    grad_out[...] = held[1, 32:64, :]
    virt = (virt0[...] + virt1[...]) + (virt2[...] + virt3[...])
    grad_virtual[...] = virt[:, :VIRT]
    lookup = POOL_SCALE * dot3(virt, hot(member[...] == iota((128, ROWS), 0)))
    for h in range(HEADS):
        at = slice(128 * h, 128 * h + 128)
        mixed[:, at] = columns[h, 0:32, :]
        whole = columns[h, 32:64, :].astype(f32) + columns[h, 64:96, :].astype(f32)
        grad_feats[:, at] = (whole + lookup[:, at]).astype(bf16)


def array(shape, kind):
    return jax.ShapeDtypeStruct(shape, kind)


VMEM = pl.BlockSpec(memory_space=pltpu.VMEM)
SMEM = pl.BlockSpec(memory_space=pltpu.SMEM)
HBM = pl.BlockSpec(memory_space=pltpu.HBM)


def call(kernel, specs, outs, scratch=(), mib=48, **named):
    return pl.pallas_call(
        kernel,
        out_shape=outs,
        in_specs=specs,
        out_specs=jax.tree.map(lambda _: VMEM, outs),
        scratch_shapes=list(scratch),
        compiler_params=pltpu.CompilerParams(vmem_limit_bytes=mib * 1024 * 1024),
        **named,
    )


def exchange(x, axis):
    return lax.all_to_all(x, axis, split_axis=0, concat_axis=0, tiled=True)


def swap(x, axis, k):
    return lax.ppermute(x, axis, [(i, i ^ k) for i in range(lax.axis_size(axis))])


def shift(x, k):
    return lax.ppermute(x, "head", [((h + k) % HEADS, h) for h in range(HEADS)])


def shards(feats, w_qkv, w_out, virt_embed, member, expander, local_mask, cotangent):
    slab = lax.axis_index("dom").astype(i32).reshape(1)
    head = lax.axis_index("head").astype(i32).reshape(1)
    members = member.reshape(1, ROWS)
    first = call(
        pool_kernel,
        [HBM] * 3,
        array((SLABS, 8, 128), f32),
        scratch=[
            pltpu.VMEM((ROWS, WIDTH), bf16),
            pltpu.VMEM((1, ROWS), i32),
            pltpu.VMEM((2, ROWS), i32),
            pltpu.SemaphoreType.DMA((3,)),
        ],
        mib=60,
    )(feats, members, expander.T)
    feats_late, first = lax.optimization_barrier([feats, first])
    first = exchange(first, "dom")
    table, kv_weights, share, embed, query_t, grad_t, table_t = call(
        project_kernel,
        [VMEM] * 5,
        (
            array((ROWS, 128), bf16),
            array((128, WIDTH), bf16),
            array((128, WIDTH), bf16),
            array((VIRT, WIDTH), bf16),
            array((32, ROWS), bf16),
            array((32, ROWS), bf16),
            array((64, ROWS), bf16),
        ),
    )(feats_late, cotangent, jnp.transpose(w_qkv, (0, 2, 1)), w_out, virt_embed)
    second, places, state = call(
        rows_kernel,
        [SMEM] + [VMEM] * 5,
        (array((SLABS, 80, 128), bf16), array((8, ROWS), f32), array((128, WIDTH), bf16)),
        scratch=[pltpu.VMEM((ROWS, 128), f32)],
    )(slab, first, table, table_t, embed, kv_weights)
    second, share, query_t = lax.optimization_barrier([second, share, query_t])
    two = jnp.concatenate([share, swap(share, "head", 4)], axis=0)
    across = lambda rows: pl.BlockSpec((rows, TI), lambda i: (0, i))
    stats = pl.pallas_call(
        local_kernel,
        grid=(ROWS // TI,),
        out_shape=array((8, ROWS), f32),
        in_specs=[across(32), across(32), pl.BlockSpec((TI, ROWS), lambda i: (i, 0)), VMEM],
        out_specs=across(8),
        compiler_params=pltpu.CompilerParams(vmem_limit_bytes=52 * 1024 * 1024),
    )(query_t, grad_t, local_mask, table_t)
    second, two, stats = lax.optimization_barrier([exchange(second, "dom"), two, stats])
    third, parts, attended, grad_query = call(
        side_kernel,
        [VMEM] * 5,
        (
            array((SLABS, 80, 128), bf16),
            array((8, ROWS), f32),
            array((32, ROWS), f32),
            array((32, ROWS), f32),
        ),
        scratch=[pltpu.VMEM((ROWS, 128), f32)],
    )(query_t, grad_t, stats, second, places)
    local, result, out_term = call(
        attend_kernel,
        [VMEM] * 6 + [HBM] * 2,
        (array((64, ROWS), f32), array((64, ROWS), bf16), array((32, WIDTH), f32)),
        scratch=[
            pltpu.VMEM((ROWS, WIDTH), bf16),
            pltpu.VMEM((ROWS, ROWS), i32),
            pltpu.SemaphoreType.DMA((ROWS // TA + 1,)),
        ],
        mib=52,
    )(parts, attended, grad_query, query_t, grad_t, table_t, cotangent, local_mask)
    third, two, share = lax.optimization_barrier([third, two, share])
    others = [shift(share, 2), shift(share, 6), shift(two, 1), shift(two, 7)]
    third = exchange(third, "dom")
    rows, stacked, virt = call(
        gather_kernel,
        [VMEM] * 4,
        (array((HEADS, 144, 128), bf16), array((128, ROWS), bf16), array((16, 128), f32)),
        scratch=[
            pltpu.VMEM((ROWS, 128), f32),
        ],
    )(third, places, local, result)
    rows, stacked, *others = lax.optimization_barrier([rows, stacked] + others)
    rows = exchange(rows, "head")
    keep, give = call(
        partial_kernel,
        [SMEM] + [VMEM] * 5,
        (array((64, WIDTH), f32), array((64, WIDTH), f32)),
        scratch=[pltpu.VMEM((2, 64, WIDTH), f32)],
    )(slab & 1, stacked, virt, feats, state, out_term)
    keep = keep + swap(give, "dom", 1)
    keep = (keep + swap(keep, "dom", 2)) + (swap(keep, "dom", 4) + swap(keep, "dom", 6))
    rows, keep = lax.optimization_barrier([rows, keep])
    columns, virt = call(
        mix_kernel,
        [SMEM] * 2 + [VMEM] * 6 + [HBM] * 2,
        (array((HEADS, 96, 128), bf16), array((32, 128), f32)),
        scratch=[
            pltpu.VMEM((128, WIDTH), bf16),
            pltpu.VMEM((128, WIDTH), bf16),
            pltpu.VMEM((WIDTH, 128), f32),
            pltpu.SemaphoreType.DMA((2,)),
        ],
    )(head, slab & 3, rows, two, *others, feats, cotangent)
    columns = exchange(columns, "head")
    both = jnp.concatenate([keep, swap(keep, "dom", 1)], axis=0)
    both = (both + swap(both, "dom", 8)) + (swap(both, "dom", 16) + swap(both, "dom", 24))
    virts = [virt] + [swap(virt, "dom", k) for k in (1, 2, 3)]
    mixed, grad_feats, grad_qkv, grad_out, grad_virtual = call(
        finish_kernel,
        [SMEM] + [VMEM] * 7,
        (
            array((32, ROWS), bf16),
            array((32, ROWS), bf16),
            array((96, WIDTH), f32),
            array((32, WIDTH), f32),
            array((32, VIRT), f32),
        ),
        scratch=[pltpu.VMEM((2, 64, WIDTH), f32)],
    )(slab & 1, columns, both, *virts, members)
    grad_qkv = jnp.transpose(grad_qkv.reshape(3, 32, WIDTH), (0, 2, 1))
    return (mixed.T, grad_feats.T, grad_qkv, grad_out, grad_virtual.T)


def solution(mesh):
    return jax.shard_map(
        shards,
        mesh=mesh,
        in_specs=(
            P("dom", None),
            P(None, None, "head"),
            P("head", None),
            P(),
            P("dom"),
            P("dom", None),
            P("dom", None),
            P("dom", None),
        ),
        out_specs=(
            P("dom", "head"),
            P("dom", "head"),
            P(None, None, "head"),
            P("head", None),
            P(None, "head"),
        ),
        check_vma=False,
    )
```

```python
import functools

import jax
import jax.numpy as jnp
from jax import lax
from jax.experimental import pallas as pl
from jax.experimental.pallas import tpu as pltpu
from jax.sharding import PartitionSpec as P

HD = 32
VIRT = 64
SLABS = 32
HEADS = 8
ROWS = 1024
WIDTH = 256
NODES = SLABS * ROWS
BLOCK = ROWS // SLABS
SCALE = HD ** (-0.5)
POOL_SCALE = (VIRT / NODES) ** 0.5
GRAD_SCALE = NODES ** (-0.5)
TI = 256
TA = 256
MASKED = -1e30
LOG2E = 1.4426950408889634
SCALE2 = SCALE * LOG2E

f32 = jnp.float32
bf16 = jnp.bfloat16
i32 = jnp.int32


def dot(a, b):
    return jnp.dot(a, b, preferred_element_type=f32)


def dot_nt(a, b):
    return lax.dot_general(a, b, (((1,), (1,)), ((), ())), preferred_element_type=f32)


def iota(shape, dim):
    return lax.broadcasted_iota(i32, shape, dim)


def hot(cond):
    return jnp.where(cond, 1.0, 0.0).astype(bf16)


def split3(x):
    hi = x.astype(bf16)
    rest = x - hi.astype(f32)
    mid = rest.astype(bf16)
    low = (rest - mid.astype(f32)).astype(bf16)
    return hi, mid, low


def dot3(x, one_hot):
    rows = x.shape[0]
    got = dot(jnp.concatenate(split3(x), axis=0), one_hot)
    return got[:rows] + got[rows : 2 * rows] + got[2 * rows :]


def lane(shape):
    return iota(shape, len(shape) - 1)


def first_virt(slab):
    return 16 * (slab & 3) + 2 * (slab >> 2)


def branch0(shape):
    return (lane(shape) & 32) == 0


def place_rows(table):
    whole = table.astype(i32)
    hi = (whole >> 5).astype(f32).astype(bf16)
    low = (whole & 31).astype(f32).astype(bf16)
    shape = (SLABS, ROWS)
    own = (iota(shape, 1) >> 5) == iota(shape, 0)
    rows = []
    for e in range(2):
        pick = hot(iota((128, ROWS), 0) == 32 * e + (iota((128, ROWS), 1) & 31))
        full = dot(jnp.concatenate([hi, low], axis=0), pick)
        full = 32.0 * full[:SLABS] + full[SLABS:]
        rows.append(jnp.sum(jnp.where(own, full, 0.0), axis=0, keepdims=True))
    return rows


def pool_kernel(feats_at, member_at, expander_at, out, feats, member, expander, sems):
    copies = [
        pltpu.make_async_copy(source, target, sems.at[k])
        for k, (source, target) in enumerate(
            ((feats_at, feats), (member_at, member), (expander_at, expander))
        )
    ]
    for copy in copies:
        copy.start()
    copies[2].wait()
    out[...] = jnp.zeros(out.shape, f32)
    shape = (SLABS, ROWS)
    total = jnp.zeros((SLABS, 128), f32)
    for e in range(2):
        target = expander[e : e + 1, :]
        own = (iota(shape, 1) & 31) == ((iota(shape, 0) - e) & 31)
        hi = jnp.where(own, ((target >> 5) & 31).astype(f32), 0.0).astype(bf16)
        low = jnp.where(own, (target & 31).astype(f32), 0.0).astype(bf16)
        slot = hot((iota((ROWS, 128), 0) >> 5) + 32 * e == iota((ROWS, 128), 1))
        total = total + 32.0 * dot(hi, slot) + dot(low, slot)
    out[:, 4, :] = total
    copies[1].wait()
    shape = (VIRT, ROWS)
    order = iota(shape, 0)
    own = hot(member[...] == first_virt(order & 31) + (order >> 5))
    copies[0].wait()
    pooled = dot(own, feats[...])
    out[:, 0, :] = pooled[:32, :128]
    out[:, 1, :] = pooled[:32, 128:]
    out[:, 2, :] = pooled[32:, :128]
    out[:, 3, :] = pooled[32:, 128:]


def project_kernel(
    feats, cotangent, w_qkv, w_out, embed_in,
    table, kv_weights, share, embed, query_t, grad_t, table_t,
):
    embed[...] = embed_in[...]
    w_q, w_k, w_v = w_qkv[0], w_qkv[1], w_qkv[2]
    w_kv4 = jnp.concatenate([w_k, w_k, w_v, w_v], axis=0)
    kv_weights[...] = w_kv4
    share[...] = jnp.concatenate([w_q, w_k, w_v, w_out[...]], axis=0)
    table[...] = dot_nt(feats[...], w_kv4).astype(bf16)
    query_t[...] = dot_nt(w_q, feats[...]).astype(bf16)
    grad_t[...] = dot_nt(w_out[...], cotangent[...]).astype(bf16)
    table_t[...] = dot_nt(jnp.concatenate([w_k, w_v], axis=0), feats[...]).astype(bf16)


def turn_parts(x):
    turned = x.astype(f32).T
    return (
        jnp.concatenate([turned[0:32], turned[64:96]], axis=0),
        jnp.concatenate([turned[32:64], turned[96:128]], axis=0),
    )


def join_parts(parts):
    first, second = parts
    return jnp.concatenate([first[0:32], second[0:32], first[32:64], second[32:64]], axis=0)


def split_places(places):
    at = iota((256, 128), 0)
    found = []
    for place in places:
        whole = place.astype(i32)
        low = whole & 255
        cols = [hot(at == low[:, 128 * c : 128 * c + 128]) for c in range(8)]
        found.append((whole >> 8, jnp.concatenate(cols, axis=1)))
    return found


def gather_rows(found, pair):
    parts = []
    for (high, low_hot), part in zip(found, pair):
        part = part.astype(bf16)
        left = jnp.concatenate([part[:, 256 * k : 256 * k + 256] for k in range(4)], axis=0)
        got = dot(left, low_hot)
        chosen = got[192:256]
        for k in range(3):
            chosen = jnp.where(high == k, got[64 * k : 64 * k + 64], chosen)
        parts.append(chosen)
    return join_parts(parts)


def scatter_rows(found, pair):
    parts = []
    for (high, low_hot), part in zip(found, pair):
        left = jnp.concatenate([jnp.where(high == k, part, 0.0) for k in range(4)], axis=0)
        got = dot_nt(left.astype(bf16), low_hot)
        parts.append(jnp.concatenate([got[64 * k : 64 * k + 64] for k in range(4)], axis=1))
    return join_parts(parts)


def to_slabs(turned):
    return turned.T.astype(bf16).reshape(SLABS, BLOCK, 128)


def rows_kernel(slab, arrived, table, table_t, virt_embed, kv_weights, out, places, state, wide):
    row0, row1 = place_rows(arrived[:, 4, :])
    at = iota((8, ROWS), 0)
    places[...] = jnp.where(at == 0, row0, jnp.where(at == 1, row1, 0.0))
    shape = (8, VIRT)
    pick = hot((iota(shape, 1) == first_virt(slab[0]) + iota(shape, 0)) & (iota(shape, 0) < 2))
    embed = dot(pick, virt_embed[...])
    pooled = jnp.sum(arrived[...], axis=0)
    first = jnp.concatenate([pooled[0:1], pooled[1:2]], axis=1)
    second = jnp.concatenate([pooled[2:3], pooled[3:4]], axis=1)
    at = iota((8, WIDTH), 0)
    pooled = jnp.where(at == 0, first, jnp.where(at == 1, second, 0.0))
    virt_state = embed + POOL_SCALE * pooled
    at = iota((128, WIDTH), 0) - 2 * (slab[0] >> 2)
    whole = jnp.where(at == 0, virt_state[0:1], jnp.where(at == 1, virt_state[1:2], 0.0))
    state[...] = whole.astype(bf16)
    virt_state = jnp.concatenate([virt_state, jnp.zeros((8, WIDTH), f32)], axis=0).astype(bf16)
    virt_rows = dot_nt(virt_state, kv_weights[...]).astype(bf16)
    out[:, 64:80, :] = jnp.broadcast_to(virt_rows[None], (SLABS, 16, 128))
    wide[...] = table[...].astype(f32)
    leave_rows(wide, out)
    out[:, 32:64, :] = to_slabs(gather_rows(split_places((row0, row1)), (table_t[...],) * 2))


def spread_rows(arrived, at, held):
    blocks = [arrived[s, at : at + 32, :].astype(f32) for s in range(SLABS)]
    low_branch = branch0((BLOCK, 128))
    for s in range(SLABS):
        block = jnp.where(low_branch, blocks[s], blocks[(s + 1) % SLABS])
        held[pl.ds(s, BLOCK, stride=SLABS), :] = block
    return held[...]


def leave_rows(held, out):
    low_branch = branch0((BLOCK, 128))
    blocks = [held[pl.ds(s, BLOCK, stride=SLABS), :] for s in range(SLABS)]
    for s in range(SLABS):
        block = jnp.where(low_branch, blocks[s], blocks[(s - 1) % SLABS])
        out[s, 0:32, :] = block.astype(bf16)


def right_tables(table_t):
    key, value = table_t[0:32, :], table_t[32:64, :]
    at = iota((16, ROWS), 0)
    none = jnp.zeros((16, ROWS), bf16)
    less_base = jnp.where(at < 3, -1.0, 0.0).astype(bf16)
    less_centre = jnp.where((at >= 3) & (at < 6), -1.0, 0.0).astype(bf16)
    keys = jnp.concatenate([key, key, key, less_base, none], axis=0)
    values = jnp.concatenate([none, none, none, none, value, less_centre, none], axis=0)
    return keys, values


def left_query(query, parts):
    wide = [part.astype(f32) for part in split3(query.astype(f32) * SCALE2)]
    rest = jnp.zeros((24, query.shape[1]), f32)
    return jnp.concatenate(wide + [parts, rest], axis=0).T.astype(bf16)


def left_grad(grad, parts):
    rest = jnp.zeros((24, grad.shape[1]), f32)
    front = jnp.zeros((64, grad.shape[1]), f32)
    return jnp.concatenate([front, grad.astype(f32), parts, rest], axis=0).T.astype(bf16)


def stack_rows(rows, fill):
    at = iota((8, ROWS), 0)
    block = jnp.full((8, ROWS), fill, f32)
    for k, row in enumerate(rows):
        block = jnp.where(at == k, row, block)
    return block


def local_kernel(query_t, grad_t, mask, table_t, stats):
    none = jnp.zeros((8, TI), f32)
    q_own = left_query(query_t[...], none)
    g_own = left_grad(grad_t[...], none)
    keys, values = right_tables(table_t)
    scores = jnp.where(mask[...] > 0, dot(q_own, keys), MASKED)
    highest = jnp.max(scores, axis=1, keepdims=True)
    weight = jnp.exp2(scores - highest)
    value_dots = dot(g_own, values)
    total = jnp.sum(weight, axis=1, keepdims=True)
    centre = jnp.sum(weight * value_dots, axis=1, keepdims=True)
    at = lane((TI, 128))
    stat = jnp.where(at == 0, highest, jnp.where(at == 1, total, centre))
    stats[...] = stat.T[0:8]


def side_kernel(
    query_t, grad_t, stats, arrived, places,
    out, parts_out, attended_out, grad_query_out,
    near,
):
    virt_rows = arrived[:, 64:80, :].astype(f32)
    pieces = [virt_rows[4 * ((v & 15) >> 1) + (v >> 4), 0:2, :] for v in range(0, VIRT, 2)]
    virt_rows = jnp.concatenate(pieces, axis=0)
    at = lane((VIRT, 128))
    virt_left = jnp.where(at < 64, virt_rows, 0.0), jnp.where(at >= 64, virt_rows, 0.0)
    virt_left = jnp.concatenate(virt_left, axis=0).astype(bf16)
    virt_t = jnp.concatenate([virt_rows, jnp.zeros((64, 128), f32)], axis=0).T.astype(bf16)
    found = split_places((places[0:1, :], places[1:2, :]))
    forward = spread_rows(arrived, 32, near).T
    inverse = scatter_rows(found, turn_parts(arrived[:, 0:32, :].reshape(ROWS, 128)))
    side_k = (forward[0:32], forward[32:64], inverse[0:32], inverse[32:64])
    side_v = (forward[64:96], forward[96:128], inverse[64:96], inverse[96:128])
    q_t, g_t = query_t[...], grad_t[...]
    q_wide, g_wide = q_t.astype(f32), g_t.astype(f32)
    none = jnp.zeros((32, ROWS), bf16)
    virt = dot(virt_left, jnp.concatenate([q_t, none, g_t, none], axis=0))
    virt_s, virt_d = SCALE2 * virt[0:VIRT], virt[VIRT:]
    side_s = [SCALE2 * jnp.sum(q_wide * part, axis=0, keepdims=True) for part in side_k]
    side_d = [jnp.sum(g_wide * part, axis=0, keepdims=True) for part in side_v]
    side_s, side_d = stack_rows(side_s, MASKED), stack_rows(side_d, 0.0)
    local_m, local_t, local_c = stats[0:1, :], stats[1:2, :], stats[2:3, :]
    highest = jnp.maximum(jnp.max(virt_s, axis=0, keepdims=True), jnp.max(side_s, axis=0, keepdims=True))
    highest = jnp.maximum(local_m, highest)
    virt_p = jnp.exp2(virt_s - highest)
    side_p = jnp.exp2(side_s - highest)
    factor = jnp.exp2(local_m - highest)
    total = factor * local_t
    total = total + jnp.sum(virt_p, axis=0, keepdims=True) + jnp.sum(side_p, axis=0, keepdims=True)
    share = 1.0 / total
    virt_p = virt_p * share
    side_p = side_p * share
    centre = factor * share * local_c + jnp.sum(virt_p * virt_d, axis=0, keepdims=True)
    centre = centre + jnp.sum(side_p * side_d, axis=0, keepdims=True)
    base = highest + LOG2E * jnp.log(total)
    parts = [part.astype(f32) for column in (base, centre) for part in split3(column)]
    parts_out[...] = stack_rows(parts, 0.0)
    virt_g = (virt_p * (virt_d - centre)).astype(bf16)
    virt_p = virt_p.astype(bf16)
    side_g = (side_p * (side_d - centre)).astype(bf16).astype(f32)
    side_p = side_p.astype(bf16).astype(f32)
    attended = dot(virt_t[64:96, 0:VIRT], virt_p)
    grad_query = dot(virt_t[0:32, 0:VIRT], virt_g)
    key_terms, value_terms = [], []
    for k in range(4):
        one_p, one_g = side_p[k : k + 1], side_g[k : k + 1]
        attended = attended + one_p * side_v[k]
        grad_query = grad_query + one_g * side_k[k]
        key_terms.append((SCALE * (one_g * q_wide)).astype(bf16).astype(f32))
        value_terms.append((one_p * g_wide).astype(bf16).astype(f32))
    near[...] = jnp.concatenate(key_terms[:2] + value_terms[:2], axis=0).T
    leave_rows(near, out)
    pair = [jnp.concatenate([key_terms[k], value_terms[k]], axis=0) for k in (2, 3)]
    out[:, 32:64, :] = to_slabs(gather_rows(found, pair))
    sums = jnp.concatenate([SCALE * dot_nt(q_t, virt_g), dot_nt(g_t, virt_p)], axis=0)
    hi = sums.astype(bf16).astype(f32)
    both_parts = jnp.concatenate([hi, sums - hi], axis=0)
    both_parts = jnp.concatenate([both_parts, jnp.zeros((128, 64), f32)], axis=1).T[0:VIRT]
    both_parts = both_parts.astype(bf16)
    for slab in range(SLABS):
        first = 16 * (slab & 3)
        out[slab, 64:80, :] = both_parts[first : first + 16]
    attended_out[...] = attended
    grad_query_out[...] = grad_query


def attend_kernel(
    parts, attended, grad_query, query_t, grad_t, table_t, cotangent_at, mask_at,
    local, result, out_term,
    cotangent, mask, sems,
):
    tiles = ROWS // TA
    copies = []
    for tile in range(tiles):
        span = pl.ds(tile * TA, TA)
        copies.append(pltpu.make_async_copy(mask_at.at[span], mask.at[span], sems.at[tile]))
    copies.append(pltpu.make_async_copy(cotangent_at, cotangent, sems.at[tiles]))
    for copy in copies:
        copy.start()
    all_keys, all_values = right_tables(table_t)
    q_t, g_t = query_t[...], grad_t[...]
    q_own = left_query(q_t, parts[...])
    g_own = left_grad(g_t, parts[...])
    key_t, value_t = table_t[0:32, :], table_t[32:64, :]
    grad_k = jnp.zeros((32, ROWS), f32)
    grad_v = jnp.zeros((32, ROWS), f32)
    for tile in range(tiles):
        span = slice(tile * TA, tile * TA + TA)
        copies[tile].wait()
        scores = jnp.where(mask[span, :] > 0, dot(q_own[span], all_keys), MASKED)
        weight = jnp.exp2(scores)
        local_p = weight.astype(bf16)
        local_g = (weight * dot(g_own[span], all_values)).astype(bf16)
        result[0:32, span] = (SCALE * (grad_query[:, span] + dot_nt(key_t, local_g))).astype(bf16)
        result[32:64, span] = (attended[:, span] + dot_nt(value_t, local_p)).astype(bf16)
        grad_k = grad_k + dot(q_t[:, span], local_g)
        grad_v = grad_v + dot(g_t[:, span], local_p)
    local[0:32, :] = SCALE * grad_k
    local[32:64, :] = grad_v
    copies[tiles].wait()
    out_term[...] = GRAD_SCALE * dot(result[32:64, :], cotangent[...])


def gather_kernel(arrived, places, local, result, rows_out, stacked_out, virt_out, near):
    found = split_places((places[0:1, :], places[1:2, :]))
    forward = scatter_rows(found, turn_parts(arrived[:, 0:32, :].reshape(ROWS, 128)))
    side = forward + spread_rows(arrived, 32, near).T
    keys_grad = (local[0:32, :] + side[0:32] + side[32:64]).astype(bf16)
    values_grad = (local[32:64, :] + side[64:96] + side[96:128]).astype(bf16)
    stacked = jnp.concatenate([result[0:32, :], keys_grad, values_grad, result[32:64, :]], axis=0)
    stacked_out[...] = stacked
    rows_out[:, 0:128, :] = stacked.astype(f32).T.astype(bf16).reshape(HEADS, 128, 128)
    parts = jnp.sum(arrived[:, 64:80, :].astype(f32), axis=0)
    virt = (parts + pltpu.roll(parts, 64, 1)).astype(bf16).astype(f32)
    inner = (lane((16, 128)) >= 32) & (lane((16, 128)) < 96)
    virt = jnp.where(inner, pltpu.roll(virt, 32, 1), 0.0)
    virt_out[...] = virt
    rows_out[:, 128:144, :] = jnp.broadcast_to(virt.astype(bf16)[None], (HEADS, 16, 128))


def partial_kernel(core, stacked, virt, feats, state, out_term, keep, give, held):
    virt = jnp.concatenate([virt[...], jnp.zeros((112, 128), f32)], axis=0)
    grads = dot(stacked[...], feats[...]) + dot(virt.T.astype(bf16), state[...])
    held[0] = GRAD_SCALE * grads[0:64]
    held[1, 0:32, :] = GRAD_SCALE * grads[64:96]
    held[1, 32:64, :] = out_term[...]
    keep[...] = held[core[0]]
    give[...] = held[1 - core[0]]


def mix_kernel(
    head, group, rows, weights0, weights2, weights6, weights1, weights7, feats_at, cotangent_at,
    columns, virt_out, feats, cotangent, turned, sems,
):
    which = head[0]
    span = pl.ds(pl.multiple_of(which * 128, 128), 128)
    copies = [
        pltpu.make_async_copy(feats_at.at[span], feats, sems.at[0]),
        pltpu.make_async_copy(cotangent_at.at[span], cotangent, sems.at[1]),
    ]
    for copy in copies:
        copy.start()
    grads = jnp.zeros((144, WIDTH), f32)
    mixed = jnp.zeros((128, WIDTH), f32)
    inner = lane((144, 128)) < 96
    sources = {0: weights0, 4: weights0, 1: weights1, 5: weights1, 7: weights7, 3: weights7}
    sources.update({2: weights2, 6: weights6})
    turns = list(sources)
    for two in (turns[0:2], turns[2:4], turns[4:6], turns[6:8]):
        found = [rows[(which + turn) & 7] for turn in two]
        zero = jnp.zeros_like(found[0])
        weight = [sources[turn][pl.ds(128 if turn in (3, 4, 5) else 0, 128), :] for turn in two]
        weight = jnp.concatenate(weight, axis=0)
        left = jnp.concatenate([jnp.where(inner, row, zero) for row in found], axis=1)
        grads = grads + dot(left, weight)
        left = jnp.concatenate([jnp.where(inner, zero, row)[0:128] for row in found], axis=1)
        mixed = mixed + dot(left, weight)
    turned[...] = jnp.concatenate([grads[128:144], jnp.zeros((112, WIDTH), f32)], axis=0).T
    own = turned[pl.ds(pl.multiple_of(which * 32, 32), 32), :]
    virt_out[...] = pltpu.roll(own, 16 * group[0], 1)
    for copy in copies:
        copy.wait()
    grads = (cotangent[...].astype(f32) + grads[0:128]).T
    mixed = (feats[...].astype(f32) + mixed).T.astype(bf16)
    hi = grads.astype(bf16)
    low = (grads - hi.astype(f32)).astype(bf16)
    columns[:, 0:32, :] = mixed.reshape(HEADS, 32, 128)
    columns[:, 32:64, :] = hi.reshape(HEADS, 32, 128)
    columns[:, 64:96, :] = low.reshape(HEADS, 32, 128)


def finish_kernel(
    core, columns, near, far, virt0, virt1, member,
    mixed, grad_feats, grad_qkv, grad_out, grad_virtual, held,
):
    held[core[0]] = near[...]
    held[1 - core[0]] = far[...]
    grad_qkv[0:64, :] = held[0]
    grad_qkv[64:96, :] = held[1, 0:32, :]
    grad_out[...] = held[1, 32:64, :]
    virt = virt0[...] + virt1[...]
    grad_virtual[...] = virt[:, :VIRT]
    lookup = POOL_SCALE * dot3(virt, hot(member[...] == iota((128, ROWS), 0)))
    for h in range(HEADS):
        at = slice(128 * h, 128 * h + 128)
        mixed[:, at] = columns[h, 0:32, :]
        whole = columns[h, 32:64, :].astype(f32) + columns[h, 64:96, :].astype(f32)
        grad_feats[:, at] = (whole + lookup[:, at]).astype(bf16)


def array(shape, kind):
    return jax.ShapeDtypeStruct(shape, kind)


VMEM = pl.BlockSpec(memory_space=pltpu.VMEM)
SMEM = pl.BlockSpec(memory_space=pltpu.SMEM)
HBM = pl.BlockSpec(memory_space=pltpu.HBM)


def call(kernel, specs, outs, scratch=(), mib=48, **named):
    return pl.pallas_call(
        kernel,
        out_shape=outs,
        in_specs=specs,
        out_specs=jax.tree.map(lambda _: VMEM, outs),
        scratch_shapes=list(scratch),
        compiler_params=pltpu.CompilerParams(vmem_limit_bytes=mib * 1024 * 1024),
        **named,
    )


def exchange(x, axis):
    return lax.all_to_all(x, axis, split_axis=0, concat_axis=0, tiled=True)


def swap(x, axis, k):
    return lax.ppermute(x, axis, [(i, i ^ k) for i in range(lax.axis_size(axis))])


def shift(x, k):
    return lax.ppermute(x, "head", [((h + k) % HEADS, h) for h in range(HEADS)])


def shards(feats, w_qkv, w_out, virt_embed, member, expander, local_mask, cotangent):
    slab = lax.axis_index("dom").astype(i32).reshape(1)
    head = lax.axis_index("head").astype(i32).reshape(1)
    members = member.reshape(1, ROWS)
    first = call(
        pool_kernel,
        [HBM] * 3,
        array((SLABS, 8, 128), f32),
        scratch=[
            pltpu.VMEM((ROWS, WIDTH), bf16),
            pltpu.VMEM((1, ROWS), i32),
            pltpu.VMEM((2, ROWS), i32),
            pltpu.SemaphoreType.DMA((3,)),
        ],
        mib=60,
    )(feats, members, expander.T)
    feats_late, first = lax.optimization_barrier([feats, first])
    first = exchange(first, "dom")
    table, kv_weights, share, embed, query_t, grad_t, table_t = call(
        project_kernel,
        [VMEM] * 5,
        (
            array((ROWS, 128), bf16),
            array((128, WIDTH), bf16),
            array((128, WIDTH), bf16),
            array((VIRT, WIDTH), bf16),
            array((32, ROWS), bf16),
            array((32, ROWS), bf16),
            array((64, ROWS), bf16),
        ),
    )(feats_late, cotangent, jnp.transpose(w_qkv, (0, 2, 1)), w_out, virt_embed)
    second, places, state = call(
        rows_kernel,
        [SMEM] + [VMEM] * 5,
        (array((SLABS, 80, 128), bf16), array((8, ROWS), f32), array((128, WIDTH), bf16)),
        scratch=[pltpu.VMEM((ROWS, 128), f32)],
    )(slab, first, table, table_t, embed, kv_weights)
    second, share, query_t = lax.optimization_barrier([second, share, query_t])
    two = jnp.concatenate([share, swap(share, "head", 4)], axis=0)
    across = lambda rows: pl.BlockSpec((rows, TI), lambda i: (0, i))
    stats = pl.pallas_call(
        local_kernel,
        grid=(ROWS // TI,),
        out_shape=array((8, ROWS), f32),
        in_specs=[across(32), across(32), pl.BlockSpec((TI, ROWS), lambda i: (i, 0)), VMEM],
        out_specs=across(8),
        compiler_params=pltpu.CompilerParams(vmem_limit_bytes=52 * 1024 * 1024),
    )(query_t, grad_t, local_mask, table_t)
    second, two, stats = lax.optimization_barrier([exchange(second, "dom"), two, stats])
    third, parts, attended, grad_query = call(
        side_kernel,
        [VMEM] * 5,
        (
            array((SLABS, 80, 128), bf16),
            array((8, ROWS), f32),
            array((32, ROWS), f32),
            array((32, ROWS), f32),
        ),
        scratch=[pltpu.VMEM((ROWS, 128), f32)],
    )(query_t, grad_t, stats, second, places)
    local, result, out_term = call(
        attend_kernel,
        [VMEM] * 6 + [HBM] * 2,
        (array((64, ROWS), f32), array((64, ROWS), bf16), array((32, WIDTH), f32)),
        scratch=[
            pltpu.VMEM((ROWS, WIDTH), bf16),
            pltpu.VMEM((ROWS, ROWS), i32),
            pltpu.SemaphoreType.DMA((ROWS // TA + 1,)),
        ],
        mib=52,
    )(parts, attended, grad_query, query_t, grad_t, table_t, cotangent, local_mask)
    third, two, share = lax.optimization_barrier([third, two, share])
    others = [shift(share, 2), shift(share, 6), shift(two, 1), shift(two, 7)]
    third = exchange(third, "dom")
    rows, stacked, virt = call(
        gather_kernel,
        [VMEM] * 4,
        (array((HEADS, 144, 128), bf16), array((128, ROWS), bf16), array((16, 128), f32)),
        scratch=[
            pltpu.VMEM((ROWS, 128), f32),
        ],
    )(third, places, local, result)
    rows, stacked, *others = lax.optimization_barrier([rows, stacked] + others)
    rows = exchange(rows, "head")
    keep, give = call(
        partial_kernel,
        [SMEM] + [VMEM] * 5,
        (array((64, WIDTH), f32), array((64, WIDTH), f32)),
        scratch=[pltpu.VMEM((2, 64, WIDTH), f32)],
    )(slab & 1, stacked, virt, feats, state, out_term)
    keep = keep + swap(give, "dom", 1)
    keep = (keep + swap(keep, "dom", 2)) + (swap(keep, "dom", 4) + swap(keep, "dom", 6))
    rows, keep = lax.optimization_barrier([rows, keep])
    columns, virt = call(
        mix_kernel,
        [SMEM] * 2 + [VMEM] * 6 + [HBM] * 2,
        (array((HEADS, 96, 128), bf16), array((32, 128), f32)),
        scratch=[
            pltpu.VMEM((128, WIDTH), bf16),
            pltpu.VMEM((128, WIDTH), bf16),
            pltpu.VMEM((WIDTH, 128), f32),
            pltpu.SemaphoreType.DMA((2,)),
        ],
    )(head, slab & 3, rows, two, *others, feats, cotangent)
    columns, keep = lax.optimization_barrier([columns, keep])
    columns = exchange(columns, "head")
    keep = (keep + swap(keep, "dom", 8)) + (swap(keep, "dom", 16) + swap(keep, "dom", 24))
    virt = virt + swap(virt, "dom", 1)
    virts = [virt, swap(virt, "dom", 2)]
    mixed, grad_feats, grad_qkv, grad_out, grad_virtual = call(
        finish_kernel,
        [SMEM] + [VMEM] * 6,
        (
            array((32, ROWS), bf16),
            array((32, ROWS), bf16),
            array((96, WIDTH), f32),
            array((32, WIDTH), f32),
            array((32, VIRT), f32),
        ),
        scratch=[pltpu.VMEM((2, 64, WIDTH), f32)],
    )(slab & 1, columns, keep, swap(keep, "dom", 1), *virts, members)
    grad_qkv = jnp.transpose(grad_qkv.reshape(3, 32, WIDTH), (0, 2, 1))
    return (mixed.T, grad_feats.T, grad_qkv, grad_out, grad_virtual.T)


def solution(mesh):
    return jax.shard_map(
        shards,
        mesh=mesh,
        in_specs=(
            P("dom", None),
            P(None, None, "head"),
            P("head", None),
            P(),
            P("dom"),
            P("dom", None),
            P("dom", None),
            P("dom", None),
        ),
        out_specs=(
            P("dom", "head"),
            P("dom", "head"),
            P(None, None, "head"),
            P("head", None),
            P(None, "head"),
        ),
        check_vma=False,
    )
```
